32 devices in a mesh: lat: 4 (over x, core), lev: 8 (over z, y).
Axes of the slice: x: 2, y: 2, z: 4, core: 2. Of those that a mesh axis runs over, the one named last changes fastest.
Arguments:
- fields: bfloat16 [6, 16, 32, 1152], P(None, 'lev', 'lat'), may hold values from -6 to 6
- courant: bfloat16 [16, 32, 1152], P('lev', 'lat'), may hold values from -0.8984375 to 0.8984375
- filter_matrix: bfloat16 [1152, 1152], replicated, may hold values from -0.1875 to 0.1875
- polar_mask: int32 [32], P('lat'), may hold values from 0 to 1, as said below
- band_start: int32 [16], replicated, may hold values from 0 to 12, as said below
- remap_weights: float32 [32, 16, 4], P('lat'), may hold values from 0.05 to 0.5
Outputs:
- remapped: bfloat16 [6, 16, 32, 1152], P(None, 'lev', 'lat')
The draws below stay inside these ranges and needn't reach their ends.
Inputs may be any that keep to these rules, and one draw needn't show every extreme that they name: `polar_mask`: 1 on a run of 4 to 8 latitudes at each pole, 0 elsewhere. band_start[0] is 0 and band_start[15] is 12.
All inputs are finite; a program needn't handle non-finite values.
Results may differ from the reference program's by a relative error of at most 0.0052.
Values may be sent and summed in bfloat16 or wider, within the bound.
No kernel may reach another device: no remote copies, remote signals or barrier semaphores. Data moves between devices by JAX's collectives and lax.ppermute only.
A program may use at most 64 MiB of HBM per device.

```python
import jax
import jax.numpy as jnp
from jax import lax

NLON = 1152
F = 6
BAND = 4
NLAT = 32
NLEV = 16
DRIFT = 4


def draw_polar_mask(key, part):
    key_south, key_north = jax.random.split(key)
    cut_south = jax.random.randint(key_south, (), NLAT // 8, NLAT // 4 + 1)
    cut_north = jax.random.randint(key_north, (), NLAT // 8, NLAT // 4 + 1)
    row_index = jnp.arange(NLAT, dtype=jnp.int32)
    return ((row_index < cut_south) | (row_index >= NLAT - cut_north)).astype(jnp.int32)


def draw_band_start(key, part):
    drift_draw = jax.random.randint(key, (NLEV,), -DRIFT, DRIFT + 1)
    level_index = jnp.arange(NLEV, dtype=jnp.int32)
    start_level = jnp.clip(level_index + drift_draw, 0, NLEV - BAND)
    start_level = start_level.at[0].set(0).at[NLEV - 1].set(NLEV - BAND)
    return start_level.astype(jnp.int32)


def level_of(key, shape, cuts, low, top_value):
    def one(dim, shards_of):
        heights = jax.random.uniform(jax.random.fold_in(jax.random.fold_in(key, 6), dim), (shards_of,), jnp.float32, low / len(cuts), top_value / len(cuts))
        return jnp.repeat(jnp.exp(heights), shape[dim] // shards_of).reshape((-1,) + (1,) * (len(shape) - dim - 1))

    level = one(*cuts[0])
    for cut in cuts[1:]:
        level = level * one(*cut)
    return level


def gaussian(own_key, shape, width, limit, cuts=(), held_as=jnp.bfloat16):
    level = level_of(own_key, shape, cuts, -0.22, 0.18) if cuts else 1.0
    values = jax.random.normal(own_key, shape, jnp.float32) * width * level
    return jnp.minimum(jnp.maximum(values, -limit), limit).astype(held_as)


def setup_inputs(seed: int = 0) -> dict:
    seeds = jax.random.split(jax.random.key(seed), 7)
    fields = gaussian(seeds[0], (F, NLEV, NLAT, NLON), 1.0, 6.0, ((1, 8), (2, 4)))
    courant = jnp.clip(jax.random.uniform(seeds[1], (NLEV, NLAT, NLON), jnp.float32, -0.8984375, 0.8984375) * level_of(seeds[1], (NLEV, NLAT, NLON), ((0, 8), (1, 4)), -0.4, 0.0), -0.8984375, 0.8984375).astype(jnp.bfloat16)
    filter_matrix = gaussian(seeds[2], (NLON, NLON), NLON ** -0.5, 0.1875)
    polar_mask = draw_polar_mask(jax.random.fold_in(seeds[6], 71), 0)
    band_start = draw_band_start(jax.random.fold_in(seeds[6], 71), 0)
    remap_weights = jnp.clip(0.05 + 0.45 * jax.random.uniform(seeds[5], (NLAT, NLEV, BAND), jnp.float32) ** level_of(seeds[5], (NLAT, NLEV, BAND), ((0, 4),), -0.2, 0.2), 0.05, 0.5)
    return {"fields": fields, "courant": courant, "filter_matrix": filter_matrix, "polar_mask": polar_mask, "band_start": band_start, "remap_weights": remap_weights}


def band_matrix(band_start, remap_weights):
    level_total = band_start.shape[0]
    band_width = remap_weights.shape[2]
    source_level = jnp.arange(level_total, dtype=jnp.int32)[None, :, None]
    target_start = band_start.astype(jnp.int32)[None, None, :] + jnp.arange(band_width, dtype=jnp.int32)[:, None, None]
    one_hot = (source_level == target_start).astype(jnp.float32)
    return jnp.einsum("jtb,bst->jst", remap_weights.astype(jnp.float32), one_hot, precision=lax.Precision.HIGHEST)


def reference(fields, courant, filter_matrix, polar_mask, band_start, remap_weights):
    lat_total = fields.shape[2]
    lon_total = fields.shape[3]
    speed_pad = jnp.pad(courant.astype(jnp.float32), ((0, 0), (2, 2), (0, 0)))
    face_index = jnp.arange(lat_total + 1, dtype=jnp.int32) - 1
    face_live = ((face_index >= 0) & (face_index <= lat_total - 2)).astype(jnp.float32)[None, :, None]
    face_speed = 0.5 * (speed_pad[:, 1:lat_total + 2] + speed_pad[:, 2:lat_total + 3]) * face_live
    matrix = band_matrix(band_start, remap_weights)
    polar_rows = (polar_mask == 1)[None, :, None]

    def one_field(field_in):
        padded = jnp.pad(field_in.astype(jnp.float32), ((0, 0), (2, 2), (0, 0)))
        face_flux = face_speed * (7.0 * (padded[:, 1:lat_total + 2] + padded[:, 2:lat_total + 3])
                                  - (padded[:, 0:lat_total + 1] + padded[:, 3:lat_total + 4])) / 12.0
        moved_field = padded[:, 2:lat_total + 2] - (face_flux[:, 1:] - face_flux[:, :-1])
        moved_low = moved_field.astype(jnp.bfloat16)
        correction = jnp.dot(moved_low.reshape(-1, lon_total), filter_matrix,
                             preferred_element_type=jnp.float32).reshape(moved_field.shape)
        filtered = (moved_field + jnp.where(polar_rows, correction, 0.0)).astype(jnp.bfloat16)
        result = jnp.einsum("sji,jst->tji", filtered.astype(jnp.float32), matrix, precision=lax.Precision.HIGHEST)
        return result.astype(jnp.bfloat16)

    return lax.map(one_field, fields)
```

```python
import functools

import jax
import jax.numpy as jnp
from jax import lax
from jax.experimental import pallas as pl
from jax.experimental.pallas import tpu as pltpu
from jax.sharding import PartitionSpec as P

WIDTH = 2
LANES = 128
EDGE_ROWS = 32
PARTS = 2
VMEM_LIMIT = 48 * 1024 * 1024
WHOLE = pl.BlockSpec(memory_space=pltpu.VMEM)


def cost(flops, moved):
    return pl.CostEstimate(flops=flops, bytes_accessed=moved, transcendentals=0)


def params():
    return pltpu.CompilerParams(vmem_limit_bytes=VMEM_LIMIT)


def exchange_order(count):
    order = list(range(count - 2, -1, -2)) + list(range(1, count, 2))
    return order[-3:] + order[:-3]


def member_at(position, count):
    member = jnp.zeros_like(position)
    for place, index in enumerate(exchange_order(count)):
        member = jnp.where(position == place, index, member)
    return member


def in_hbm(array):
    return pltpu.with_memory_space_constraint(array, pltpu.HBM)


def in_vmem(array):
    return pltpu.with_memory_space_constraint(array, pltpu.VMEM)


def iota(shape, axis):
    return lax.broadcasted_iota(jnp.int32, shape, axis)


def edge_shape(field_edges, levels, lon):
    pieces = max(p for p in range(1, 8 // levels + 1) if lon // LANES % p == 0)
    return 8, field_edges // 8 * lon + lon // pieces


def write_edges(ref, edges, field_edges, levels):
    lon = edges.shape[1]
    groups = field_edges // 8
    for group in range(groups):
        part = edges[group * 8 : group * 8 + 8]
        ref[:, group * lon : (group + 1) * lon] = part.astype(jnp.bfloat16)
    width = ref.shape[1] - groups * lon
    courant = edges[field_edges : field_edges + levels]
    parts = [courant[:, at : at + width] for at in range(0, lon, width)]
    rest = 8 - len(parts) * levels
    if rest:
        parts.append(jnp.zeros((rest, width), jnp.float32))
    ref[:, groups * lon :] = jnp.concatenate(parts, axis=0).astype(jnp.bfloat16)


def read_edges(ref, field_edges, levels, lon):
    groups = field_edges // 8
    edges = ref[...].astype(jnp.float32)
    fields = [edges[:, group * lon : (group + 1) * lon] for group in range(groups)]
    width = edges.shape[1] - groups * lon
    courant = [
        edges[part * levels : (part + 1) * levels, groups * lon :] for part in range(lon // width)
    ]
    return fields, jnp.concatenate(courant, axis=1)


def write_stencil(stencil_ref, field_count, levels, rows):
    count = field_count * levels * rows
    speed_count = levels * rows
    lat = lax.axis_index("lat")
    lats = lax.axis_size("lat")
    odd = lat % 2

    own = (field_count + 1) * speed_count
    field_edges = field_count * levels * WIDTH
    column = iota((1, stencil_ref.shape[1]), 1)
    edge = column - own
    speed_edge = edge - 2 * field_edges
    is_own, is_speed = edge < 0, speed_edge >= 0
    far = jnp.where(is_speed, speed_edge // levels, edge // field_edges)
    field_edge = edge - far * field_edges
    edge_block = jnp.where(
        is_speed, speed_edge - far * levels + field_count * levels, field_edge // WIDTH
    )
    sides = jnp.where((lat > 0) & (lat < lats - 1), 2, 1)
    block = jnp.where(is_own, column // rows, jnp.where(far < sides, edge_block, -1))
    high = (odd + far + 1) % 2
    edge_place = jnp.where(is_speed, high * (rows + 1) - 1, field_edge % WIDTH - WIDTH + high * (rows + WIDTH))
    place = jnp.where(is_own, column % rows, edge_place)

    def relation(height, first_block):
        line = iota((height, 1), 0)
        line_block = line // rows
        row = line - line_block * rows
        return row, place - row, block == line_block + first_block

    def near_face(here, shift):
        return (here == shift) | (here == shift - 1)

    _, here, same = relation(count, 0)
    for side in range(2):
        outer = (here == side + 1) | (here == side - 2)
        value = jnp.where(near_face(here, side), 7.0, jnp.where(outer, -1.0, 0.0))
        stencil_ref[side * count : (side + 1) * count] = jnp.where(same, value, 0.0).astype(
            jnp.bfloat16
        )
    row, here, same = relation(speed_count, field_count * levels)
    live = ((row > 0) | (lat > 0), (row < rows - 1) | (lat < lats - 1))
    for side in range(2):
        first = 2 * count + side * speed_count
        value = jnp.where(same & near_face(here, side) & live[side], 0.5, 0.0)
        stencil_ref[first : first + speed_count] = value.astype(jnp.bfloat16)


def write_band_matrix(band_matrix_ref, polar_ref, mask_ref, band_ref, weight_ref, rows, levels):
    polar_row = iota(polar_ref.shape, 0)
    polar = jnp.zeros(polar_ref.shape, jnp.int32)
    for index in range(rows):
        polar = jnp.where(polar_row == index, mask_ref[:, index : index + 1], polar)
    polar_ref[...] = polar

    band_width, level_total = weight_ref.shape[1:]
    total = level_total * rows

    def level_at(index):
        place = index // rows
        position = place // levels
        return (member_at(position, level_total // levels) - position) * levels + place

    out_row, in_row = iota((total, 1), 0), iota((1, total), 1)
    of_row = level_at(out_row) == iota((1, level_total), 1)

    def spread(table):
        whole = jnp.concatenate([table] * level_total, axis=0)
        return jnp.sum(jnp.where(of_row, whole, jnp.zeros_like(whole)), axis=1, keepdims=True)

    start = spread(jnp.broadcast_to(band_ref[...], (rows, level_total)))
    offset = level_at(in_row) - start
    matrix = jnp.zeros((total, total), jnp.float32)
    for band in range(band_width):
        matrix = jnp.where(offset == band, spread(weight_ref[:, band, :]), matrix)
    matrix = jnp.where(in_row % rows == out_row % rows, matrix, 0.0)
    for part in range(PARTS):
        rounded = matrix.astype(jnp.bfloat16)
        band_matrix_ref[part * total : (part + 1) * total] = rounded
        matrix = matrix - rounded.astype(jnp.float32)


def edges_body(
    filter_hbm, fields_hbm, courant_hbm, mask_hbm, band_hbm, weight_hbm,
    near_ref, far_ref, stack_ref, stencil_ref, polar_ref, band_matrix_ref,
    mask_ref, band_ref, weight_ref, sems,
    *, field_count, levels, rows
):
    own = stack_ref.shape[0]
    blocks = own // rows
    field_rows = field_count * levels * rows
    pairs = (
        (fields_hbm, stack_ref.at[pl.ds(0, field_rows)]),
        (courant_hbm, stack_ref.at[pl.ds(field_rows, own - field_rows)]),
        (weight_hbm, weight_ref),
        (band_hbm, band_ref),
        (mask_hbm, mask_ref),
    )
    copies = [
        pltpu.make_async_copy(source, target, sems.at[index])
        for index, (source, target) in enumerate(pairs)
    ]
    for copy in copies:
        copy.start()
    odd = lax.axis_index("lat") % 2
    edge = iota((2 * EDGE_ROWS, 1), 0)
    far = (edge >= EDGE_ROWS).astype(jnp.int32)
    inner = edge - far * EDGE_ROWS
    high = (odd + far + 1) % 2
    field_edges = field_count * levels * WIDTH
    of_field = inner < field_edges
    block = jnp.where(of_field, inner // WIDTH, inner - field_edges + field_count * levels)
    row = jnp.where(of_field, inner % WIDTH + high * (rows - WIDTH), high * (rows - 1))
    wanted = jnp.where(block < blocks, block * rows + row, -1)
    pick = jnp.where(iota((2 * EDGE_ROWS, own), 1) == wanted, 1.0, 0.0).astype(jnp.bfloat16)
    write_stencil(stencil_ref, field_count, levels, rows)
    for copy in copies[2:]:
        copy.wait()
    write_band_matrix(band_matrix_ref, polar_ref, mask_ref, band_ref, weight_ref, rows, levels)
    for copy in copies[:2]:
        copy.wait()
    edges = jnp.dot(pick, stack_ref[...], preferred_element_type=jnp.float32)
    write_edges(near_ref, edges[:EDGE_ROWS], field_edges, levels)
    for member in range(2):
        write_edges(far_ref.at[member], edges[EDGE_ROWS:], field_edges, levels)


def tiles(field_count, levels, lon, units):
    for field in range(field_count):
        for part in range(lon // LANES):
            unit = field * (lon // LANES) + part
            for level in range(levels):
                yield field, level, part * LANES, (unit // units, unit % units, level)


def transport_body(
    near_ref, far_ref, stack_ref, stencil_ref, filter_ref, polar_ref, out_ref, *, field_count
):
    pieces, units, levels, rows, _ = out_ref.shape
    lon = stack_ref.shape[1]
    count = field_count * levels * rows
    speed_count = levels * rows
    field_edges = field_count * levels * WIDTH
    near_fields, near_courant = read_edges(near_ref, field_edges, levels, lon)
    partner = lax.axis_index("lat") % 2
    far_fields, far_courant = read_edges(far_ref.at[partner], field_edges, levels, lon)
    rest = EDGE_ROWS // 2 - 2 * levels
    speeds = [near_courant, far_courant, jnp.zeros((rest, lon), jnp.float32)]
    edges = jnp.concatenate(
        near_fields + far_fields + [jnp.concatenate(speeds, axis=0)], axis=0
    )
    source = jnp.concatenate([stack_ref[...], edges.astype(jnp.bfloat16)], axis=0)
    values = jnp.dot(stencil_ref[...], source, preferred_element_type=jnp.float32)
    speed_low = values[2 * count : 2 * count + speed_count] * (1.0 / 12.0)
    speed_high = values[2 * count + speed_count :] * (1.0 / 12.0)
    parts = []
    for first in range(0, count, speed_count):
        flux_low = speed_low * values[first : first + speed_count]
        flux_high = speed_high * values[count + first : count + first + speed_count]
        own = stack_ref[first : first + speed_count].astype(jnp.float32)
        parts.append(own - (flux_high - flux_low))
    moved = jnp.concatenate(parts, axis=0)

    def write(filtered):
        for field, level, at, place in tiles(field_count, levels, lon, units):
            first = (field * levels + level) * rows
            tile = filtered[first : first + rows, at : at + LANES]
            out_ref[place] = tile.astype(jnp.bfloat16)
        for unit in range(field_count * lon // LANES, pieces * units):
            out_ref[unit // units, unit % units] = jnp.zeros(out_ref.shape[2:], jnp.bfloat16)

    polar = polar_ref[...] == 1
    any_polar = jnp.max(polar_ref[...]) == 1

    @pl.when(any_polar)
    def _():
        correction = jnp.dot(
            moved.astype(jnp.bfloat16), filter_ref[...], preferred_element_type=jnp.float32
        )
        wide = jnp.concatenate([polar] * (lon // LANES), axis=1)
        whole = jnp.concatenate([wide] * (field_count * levels), axis=0)
        write(moved + jnp.where(whole, correction, 0.0))

    @pl.when(jnp.logical_not(any_polar))
    def _():
        write(moved)


def remap_body(band_matrix_ref, source_ref, out_ref):
    pieces, units, levels, rows, _ = source_ref.shape
    total = pieces * levels * rows
    columns = jnp.concatenate(
        [
            source_ref[:, unit].astype(jnp.float32).reshape(total, LANES).astype(jnp.bfloat16)
            for unit in range(units)
        ],
        axis=1,
    )
    split = jnp.dot(band_matrix_ref[...], columns, preferred_element_type=jnp.float32)
    result = split[(PARTS - 1) * total :]
    for part in range(PARTS - 1)[::-1]:
        result = result + split[part * total : (part + 1) * total]
    for unit in range(units):
        part = result[:, unit * LANES : (unit + 1) * LANES]
        out_ref[:, unit] = part.reshape(pieces, levels, rows, LANES).astype(jnp.bfloat16)


def collect_body(source_ref, out_hbm, out_ref, sems):
    field_count, levels, _, lon = out_ref.shape
    units = source_ref.shape[1]
    copies = []
    for field, level, at, place in tiles(field_count, levels, lon, units):
        out_ref[field, level, :, at : at + LANES] = source_ref[place]
        if at + LANES == lon and level == levels - 1:
            copy = pltpu.make_async_copy(out_ref.at[field], out_hbm.at[field], sems.at[field])
            copy.start()
            copies.append(copy)
    for copy in copies:
        copy.wait()


def on_device(fields, courant, filter_matrix, polar_mask, band_start, remap_weights):
    def array(*shape, dtype=jnp.bfloat16):
        return jax.ShapeDtypeStruct(shape, dtype)

    field_count, levels, rows, lon = fields.shape
    lats, levs = lax.axis_size("lat"), lax.axis_size("lev")
    level_total, band_width = remap_weights.shape[1:]
    if lon % LANES or rows % 8:
        raise ValueError("uneven tiles")
    units = -(-(field_count * lon // LANES) // levs)
    count = field_count * levels * rows
    blocks = (field_count + 1) * levels
    own = blocks * rows
    field_edges = field_count * levels * WIDTH
    if field_edges % 8 or 8 % levels or field_edges + levels > EDGE_ROWS:
        raise ValueError("uneven edges")
    edges = array(*edge_shape(field_edges, levels, lon))
    total = level_total * rows

    hbm = pl.BlockSpec(memory_space=pltpu.HBM)
    sizes = dict(field_count=field_count, levels=levels, rows=rows)
    small = [
        polar_mask.reshape(1, -1),
        band_start.reshape(1, -1),
        jnp.swapaxes(remap_weights, 1, 2),
    ]
    inputs = [filter_matrix, fields.reshape(count, lon), courant.reshape(own - count, lon), *small]
    near, far, stack, stencil, polar, band_matrix = pl.pallas_call(
        functools.partial(edges_body, **sizes),
        out_shape=(
            edges,
            array(2, *edges.shape),
            array(own, lon),
            array(2 * (count + levels * rows), own + 2 * field_edges + EDGE_ROWS // 2),
            array(rows, LANES, dtype=jnp.int32),
            array(PARTS * total, total),
        ),
        in_specs=[hbm] * len(inputs),
        out_specs=(WHOLE,) * 6,
        scratch_shapes=[pltpu.VMEM(each.shape, each.dtype) for each in small]
        + [pltpu.SemaphoreType.DMA((len(inputs) - 1,))],
        compiler_params=params(),
        cost_estimate=cost(2 * own * own * lon, 4 * own * lon),
    )(*map(in_hbm, inputs))

    near_pairs = [(i, i + 1) for i in range(0, lats - 1, 2)]
    from_near = lax.ppermute(
        near, "lat", near_pairs + [(target, source) for source, target in near_pairs]
    )
    far_groups = [[i, i + 1] for i in range(1, lats - 1, 2)] + [[0, lats - 1]]

    def exchange_far(array):
        return lax.all_to_all(
            array, "lat", split_axis=0, concat_axis=0, tiled=True, axis_index_groups=far_groups
        )

    lat_index = lax.axis_index("lat")
    has_far = (lat_index > 0) & (lat_index < lats - 1)
    from_far = lax.cond(has_far, exchange_far, lambda array: array, far)

    pieces = pl.pallas_call(
        functools.partial(transport_body, field_count=field_count),
        out_shape=array(levs, units, levels, rows, LANES),
        in_specs=[WHOLE] * 6,
        out_specs=WHOLE,
        compiler_params=params(),
        cost_estimate=cost(2 * count * lon * lon, 2 * lon * lon),
    )(from_near, from_far, stack, stencil, in_vmem(filter_matrix), polar)

    def exchange(array):
        group = exchange_order(levs)
        return lax.all_to_all(
            array, "lev", split_axis=0, concat_axis=0, tiled=True, axis_index_groups=[group]
        )

    remapped = pl.pallas_call(
        remap_body,
        out_shape=array(*pieces.shape),
        in_specs=[WHOLE] * 2,
        out_specs=WHOLE,
        compiler_params=params(),
        cost_estimate=cost(6 * total * total * units * LANES, 4 * total * units * LANES),
    )(band_matrix, exchange(pieces))
    return pl.pallas_call(
        collect_body,
        out_shape=array(*fields.shape),
        in_specs=[WHOLE],
        out_specs=hbm,
        scratch_shapes=[
            pltpu.VMEM(fields.shape, fields.dtype),
            pltpu.SemaphoreType.DMA((field_count,)),
        ],
        compiler_params=params(),
        cost_estimate=cost(count * lon, 4 * count * lon),
    )(exchange(remapped))


def solution(mesh):
    return jax.shard_map(
        on_device,
        mesh=mesh,
        in_specs=(
            P(None, "lev", "lat", None),
            P("lev", "lat", None),
            P(),
            P("lat"),
            P(),
            P("lat", None, None),
        ),
        out_specs=P(None, "lev", "lat", None),
        check_vma=False,
    )
```

```python
import functools

import jax
import jax.numpy as jnp
from jax import lax
from jax.experimental import pallas as pl
from jax.experimental.pallas import tpu as pltpu
from jax.sharding import PartitionSpec as P

WIDTH = 2
LANES = 128
EDGE_ROWS = 32
PARTS = 2
VMEM_LIMIT = 48 * 1024 * 1024
WHOLE = pl.BlockSpec(memory_space=pltpu.VMEM)


def cost(flops, moved):
    return pl.CostEstimate(flops=flops, bytes_accessed=moved, transcendentals=0)


def params():
    return pltpu.CompilerParams(vmem_limit_bytes=VMEM_LIMIT)


def exchange_order(count):
    order = list(range(count - 1, 0, -2)) + list(range(0, count, 2))
    return order[1:] + order[:1]


def member_at(position, count):
    member = jnp.zeros_like(position)
    for place, index in enumerate(exchange_order(count)):
        member = jnp.where(position == place, index, member)
    return member


def in_hbm(array):
    return pltpu.with_memory_space_constraint(array, pltpu.HBM)


def in_vmem(array):
    return pltpu.with_memory_space_constraint(array, pltpu.VMEM)


def iota(shape, axis):
    return lax.broadcasted_iota(jnp.int32, shape, axis)


def edge_shape(field_edges, levels, lon):
    pieces = max(p for p in range(1, 8 // levels + 1) if lon // LANES % p == 0)
    return 8, field_edges // 8 * lon + lon // pieces


def write_edges(ref, edges, field_edges, levels):
    lon = edges.shape[1]
    groups = field_edges // 8
    for group in range(groups):
        part = edges[group * 8 : group * 8 + 8]
        ref[:, group * lon : (group + 1) * lon] = part.astype(jnp.bfloat16)
    width = ref.shape[1] - groups * lon
    courant = edges[field_edges : field_edges + levels]
    parts = [courant[:, at : at + width] for at in range(0, lon, width)]
    rest = 8 - len(parts) * levels
    if rest:
        parts.append(jnp.zeros((rest, width), jnp.float32))
    ref[:, groups * lon :] = jnp.concatenate(parts, axis=0).astype(jnp.bfloat16)


def read_edges(ref, field_edges, levels, lon):
    groups = field_edges // 8
    edges = ref[...].astype(jnp.float32)
    fields = [edges[:, group * lon : (group + 1) * lon] for group in range(groups)]
    width = edges.shape[1] - groups * lon
    courant = [
        edges[part * levels : (part + 1) * levels, groups * lon :] for part in range(lon // width)
    ]
    return fields, jnp.concatenate(courant, axis=1)


def write_stencil(stencil_ref, field_count, levels, rows):
    count = field_count * levels * rows
    speed_count = levels * rows
    lat = lax.axis_index("lat")
    lats = lax.axis_size("lat")
    odd = lat % 2

    own = (field_count + 1) * speed_count
    field_edges = field_count * levels * WIDTH
    column = iota((1, stencil_ref.shape[1]), 1)
    edge = column - own
    speed_edge = edge - 2 * field_edges
    is_own, is_speed = edge < 0, speed_edge >= 0
    far = jnp.where(is_speed, speed_edge // levels, edge // field_edges)
    field_edge = edge - far * field_edges
    edge_block = jnp.where(
        is_speed, speed_edge - far * levels + field_count * levels, field_edge // WIDTH
    )
    sides = jnp.where((lat > 0) & (lat < lats - 1), 2, 1)
    block = jnp.where(is_own, column // rows, jnp.where(far < sides, edge_block, -1))
    high = (odd + far + 1) % 2
    edge_place = jnp.where(is_speed, high * (rows + 1) - 1, field_edge % WIDTH - WIDTH + high * (rows + WIDTH))
    place = jnp.where(is_own, column % rows, edge_place)

    def relation(height, first_block):
        line = iota((height, 1), 0)
        line_block = line // rows
        row = line - line_block * rows
        return row, place - row, block == line_block + first_block

    def near_face(here, shift):
        return (here == shift) | (here == shift - 1)

    _, here, same = relation(count, 0)
    for side in range(2):
        outer = (here == side + 1) | (here == side - 2)
        value = jnp.where(near_face(here, side), 7.0, jnp.where(outer, -1.0, 0.0))
        stencil_ref[side * count : (side + 1) * count] = jnp.where(same, value, 0.0).astype(
            jnp.bfloat16
        )
    row, here, same = relation(speed_count, field_count * levels)
    live = ((row > 0) | (lat > 0), (row < rows - 1) | (lat < lats - 1))
    for side in range(2):
        first = 2 * count + side * speed_count
        value = jnp.where(same & near_face(here, side) & live[side], 0.5, 0.0)
        stencil_ref[first : first + speed_count] = value.astype(jnp.bfloat16)


def write_band_matrix(band_matrix_ref, polar_ref, mask_ref, band_ref, weight_ref, rows, levels):
    polar_row = iota(polar_ref.shape, 0)
    polar = jnp.zeros(polar_ref.shape, jnp.int32)
    for index in range(rows):
        polar = jnp.where(polar_row == index, mask_ref[:, index : index + 1], polar)
    polar_ref[...] = polar

    band_width, level_total = weight_ref.shape[1:]
    total = level_total * rows

    def level_at(index):
        place = index // rows
        position = place // levels
        return (member_at(position, level_total // levels) - position) * levels + place

    out_row, in_row = iota((total, 1), 0), iota((1, total), 1)
    of_row = level_at(out_row) == iota((1, level_total), 1)

    def spread(table):
        whole = jnp.concatenate([table] * level_total, axis=0)
        return jnp.sum(jnp.where(of_row, whole, jnp.zeros_like(whole)), axis=1, keepdims=True)

    start = spread(jnp.broadcast_to(band_ref[...], (rows, level_total)))
    offset = level_at(in_row) - start
    matrix = jnp.zeros((total, total), jnp.float32)
    for band in range(band_width):
        matrix = jnp.where(offset == band, spread(weight_ref[:, band, :]), matrix)
    matrix = jnp.where(in_row % rows == out_row % rows, matrix, 0.0)
    for part in range(PARTS):
        rounded = matrix.astype(jnp.bfloat16)
        band_matrix_ref[part * total : (part + 1) * total] = rounded
        matrix = matrix - rounded.astype(jnp.float32)


def edges_body(
    filter_hbm, fields_hbm, courant_hbm, mask_hbm, band_hbm, weight_hbm,
    near_ref, far_ref, stack_ref, stencil_ref, polar_ref, band_matrix_ref,
    mask_ref, band_ref, weight_ref, sems,
    *, field_count, levels, rows
):
    own = stack_ref.shape[0]
    blocks = own // rows
    field_rows = field_count * levels * rows
    pairs = (
        (fields_hbm, stack_ref.at[pl.ds(0, field_rows)]),
        (courant_hbm, stack_ref.at[pl.ds(field_rows, own - field_rows)]),
        (weight_hbm, weight_ref),
        (band_hbm, band_ref),
        (mask_hbm, mask_ref),
    )
    copies = [
        pltpu.make_async_copy(source, target, sems.at[index])
        for index, (source, target) in enumerate(pairs)
    ]
    for copy in copies:
        copy.start()
    odd = lax.axis_index("lat") % 2
    edge = iota((2 * EDGE_ROWS, 1), 0)
    far = (edge >= EDGE_ROWS).astype(jnp.int32)
    inner = edge - far * EDGE_ROWS
    high = (odd + far + 1) % 2
    field_edges = field_count * levels * WIDTH
    of_field = inner < field_edges
    block = jnp.where(of_field, inner // WIDTH, inner - field_edges + field_count * levels)
    row = jnp.where(of_field, inner % WIDTH + high * (rows - WIDTH), high * (rows - 1))
    wanted = jnp.where(block < blocks, block * rows + row, -1)
    pick = jnp.where(iota((2 * EDGE_ROWS, own), 1) == wanted, 1.0, 0.0).astype(jnp.bfloat16)
    write_stencil(stencil_ref, field_count, levels, rows)
    for copy in copies[2:]:
        copy.wait()
    write_band_matrix(band_matrix_ref, polar_ref, mask_ref, band_ref, weight_ref, rows, levels)
    for copy in copies[:2]:
        copy.wait()
    edges = jnp.dot(pick, stack_ref[...], preferred_element_type=jnp.float32)
    write_edges(near_ref, edges[:EDGE_ROWS], field_edges, levels)
    for member in range(2):
        write_edges(far_ref.at[member], edges[EDGE_ROWS:], field_edges, levels)


def tiles(field_count, levels, lon, units):
    for field in range(field_count):
        for part in range(lon // LANES):
            unit = field * (lon // LANES) + part
            for level in range(levels):
                yield field, level, part * LANES, (unit // units, unit % units, level)


def transport_body(
    near_ref, far_ref, stack_ref, stencil_ref, filter_ref, polar_ref, out_ref, *, field_count
):
    pieces, units, levels, rows, _ = out_ref.shape
    lon = stack_ref.shape[1]
    count = field_count * levels * rows
    speed_count = levels * rows
    field_edges = field_count * levels * WIDTH
    near_fields, near_courant = read_edges(near_ref, field_edges, levels, lon)
    partner = lax.axis_index("lat") % 2
    far_fields, far_courant = read_edges(far_ref.at[partner], field_edges, levels, lon)
    rest = EDGE_ROWS // 2 - 2 * levels
    speeds = [near_courant, far_courant, jnp.zeros((rest, lon), jnp.float32)]
    edges = jnp.concatenate(
        near_fields + far_fields + [jnp.concatenate(speeds, axis=0)], axis=0
    )
    source = jnp.concatenate([stack_ref[...], edges.astype(jnp.bfloat16)], axis=0)
    values = jnp.dot(stencil_ref[...], source, preferred_element_type=jnp.float32)
    speed_low = values[2 * count : 2 * count + speed_count] * (1.0 / 12.0)
    speed_high = values[2 * count + speed_count :] * (1.0 / 12.0)
    parts = []
    for first in range(0, count, speed_count):
        flux_low = speed_low * values[first : first + speed_count]
        flux_high = speed_high * values[count + first : count + first + speed_count]
        own = stack_ref[first : first + speed_count].astype(jnp.float32)
        parts.append(own - (flux_high - flux_low))
    moved = jnp.concatenate(parts, axis=0)

    def write(filtered):
        for field, level, at, place in tiles(field_count, levels, lon, units):
            first = (field * levels + level) * rows
            tile = filtered[first : first + rows, at : at + LANES]
            out_ref[place] = tile.astype(jnp.bfloat16)
        for unit in range(field_count * lon // LANES, pieces * units):
            out_ref[unit // units, unit % units] = jnp.zeros(out_ref.shape[2:], jnp.bfloat16)

    polar = polar_ref[...] == 1
    any_polar = jnp.max(polar_ref[...]) == 1

    @pl.when(any_polar)
    def _():
        correction = jnp.dot(
            moved.astype(jnp.bfloat16), filter_ref[...], preferred_element_type=jnp.float32
        )
        wide = jnp.concatenate([polar] * (lon // LANES), axis=1)
        whole = jnp.concatenate([wide] * (field_count * levels), axis=0)
        write(moved + jnp.where(whole, correction, 0.0))

    @pl.when(jnp.logical_not(any_polar))
    def _():
        write(moved)


def remap_body(band_matrix_ref, source_ref, out_ref):
    pieces, units, levels, rows, _ = source_ref.shape
    total = pieces * levels * rows
    columns = jnp.concatenate(
        [
            source_ref[:, unit].astype(jnp.float32).reshape(total, LANES).astype(jnp.bfloat16)
            for unit in range(units)
        ],
        axis=1,
    )
    split = jnp.dot(band_matrix_ref[...], columns, preferred_element_type=jnp.float32)
    result = split[(PARTS - 1) * total :]
    for part in range(PARTS - 1)[::-1]:
        result = result + split[part * total : (part + 1) * total]
    for unit in range(units):
        part = result[:, unit * LANES : (unit + 1) * LANES]
        out_ref[:, unit] = part.reshape(pieces, levels, rows, LANES).astype(jnp.bfloat16)


def collect_body(source_ref, out_hbm, out_ref, sems):
    field_count, levels, _, lon = out_ref.shape
    units = source_ref.shape[1]
    copies = []
    for field, level, at, place in tiles(field_count, levels, lon, units):
        out_ref[field, level, :, at : at + LANES] = source_ref[place]
        if at + LANES == lon and level == levels - 1:
            copy = pltpu.make_async_copy(out_ref.at[field], out_hbm.at[field], sems.at[field])
            copy.start()
            copies.append(copy)
    for copy in copies:
        copy.wait()


def on_device(fields, courant, filter_matrix, polar_mask, band_start, remap_weights):
    def array(*shape, dtype=jnp.bfloat16):
        return jax.ShapeDtypeStruct(shape, dtype)

    field_count, levels, rows, lon = fields.shape
    lats, levs = lax.axis_size("lat"), lax.axis_size("lev")
    level_total, band_width = remap_weights.shape[1:]
    if lon % LANES or rows % 8:
        raise ValueError("uneven tiles")
    units = -(-(field_count * lon // LANES) // levs)
    count = field_count * levels * rows
    blocks = (field_count + 1) * levels
    own = blocks * rows
    field_edges = field_count * levels * WIDTH
    if field_edges % 8 or 8 % levels or field_edges + levels > EDGE_ROWS:
        raise ValueError("uneven edges")
    edges = array(*edge_shape(field_edges, levels, lon))
    total = level_total * rows

    hbm = pl.BlockSpec(memory_space=pltpu.HBM)
    sizes = dict(field_count=field_count, levels=levels, rows=rows)
    small = [
        polar_mask.reshape(1, -1),
        band_start.reshape(1, -1),
        jnp.swapaxes(remap_weights, 1, 2),
    ]
    inputs = [filter_matrix, fields.reshape(count, lon), courant.reshape(own - count, lon), *small]
    near, far, stack, stencil, polar, band_matrix = pl.pallas_call(
        functools.partial(edges_body, **sizes),
        out_shape=(
            edges,
            array(2, *edges.shape),
            array(own, lon),
            array(2 * (count + levels * rows), own + 2 * field_edges + EDGE_ROWS // 2),
            array(rows, LANES, dtype=jnp.int32),
            array(PARTS * total, total),
        ),
        in_specs=[hbm] * len(inputs),
        out_specs=(WHOLE,) * 6,
        scratch_shapes=[pltpu.VMEM(each.shape, each.dtype) for each in small]
        + [pltpu.SemaphoreType.DMA((len(inputs) - 1,))],
        compiler_params=params(),
        cost_estimate=cost(2 * own * own * lon, 4 * own * lon),
    )(*map(in_hbm, inputs))

    near_pairs = [(i, i + 1) for i in range(0, lats - 1, 2)]
    from_near = lax.ppermute(
        near, "lat", near_pairs + [(target, source) for source, target in near_pairs]
    )
    far_groups = [[i, i + 1] for i in range(1, lats - 1, 2)] + [[0, lats - 1]]

    def exchange_far(array):
        return lax.all_to_all(
            array, "lat", split_axis=0, concat_axis=0, tiled=True, axis_index_groups=far_groups
        )

    lat_index = lax.axis_index("lat")
    has_far = (lat_index > 0) & (lat_index < lats - 1)
    from_far = lax.cond(has_far, exchange_far, lambda array: array, far)

    pieces = pl.pallas_call(
        functools.partial(transport_body, field_count=field_count),
        out_shape=array(levs, units, levels, rows, LANES),
        in_specs=[WHOLE] * 6,
        out_specs=WHOLE,
        compiler_params=params(),
        cost_estimate=cost(2 * count * lon * lon, 2 * lon * lon),
    )(from_near, from_far, stack, stencil, in_vmem(filter_matrix), polar)

    def exchange(array):
        group = exchange_order(levs)
        return lax.all_to_all(
            array, "lev", split_axis=0, concat_axis=0, tiled=True, axis_index_groups=[group]
        )

    remapped = pl.pallas_call(
        remap_body,
        out_shape=array(*pieces.shape),
        in_specs=[WHOLE] * 2,
        out_specs=WHOLE,
        compiler_params=params(),
        cost_estimate=cost(6 * total * total * units * LANES, 4 * total * units * LANES),
    )(band_matrix, exchange(pieces))
    return pl.pallas_call(
        collect_body,
        out_shape=array(*fields.shape),
        in_specs=[WHOLE],
        out_specs=hbm,
        scratch_shapes=[
            pltpu.VMEM(fields.shape, fields.dtype),
            pltpu.SemaphoreType.DMA((field_count,)),
        ],
        compiler_params=params(),
        cost_estimate=cost(count * lon, 4 * count * lon),
    )(exchange(remapped))


def solution(mesh):
    return jax.shard_map(
        on_device,
        mesh=mesh,
        in_specs=(
            P(None, "lev", "lat", None),
            P("lev", "lat", None),
            P(),
            P("lat"),
            P(),
            P("lat", None, None),
        ),
        out_specs=P(None, "lev", "lat", None),
        check_vma=False,
    )
```

```python
import functools

import jax
import jax.numpy as jnp
from jax import lax
from jax.experimental import pallas as pl
from jax.experimental.pallas import tpu as pltpu
from jax.sharding import PartitionSpec as P

WIDTH = 2
LANES = 128
EDGE_ROWS = 32
PARTS = 2
VMEM_LIMIT = 48 * 1024 * 1024
WHOLE = pl.BlockSpec(memory_space=pltpu.VMEM)


def cost(flops, moved):
    return pl.CostEstimate(flops=flops, bytes_accessed=moved, transcendentals=0)


def params():
    return pltpu.CompilerParams(vmem_limit_bytes=VMEM_LIMIT)


def exchange_order(count):
    order = list(range(count))[::-1]
    return order[2:] + order[:2]


def member_at(position, count):
    member = jnp.zeros_like(position)
    for place, index in enumerate(exchange_order(count)):
        member = jnp.where(position == place, index, member)
    return member


def in_hbm(array):
    return pltpu.with_memory_space_constraint(array, pltpu.HBM)


def in_vmem(array):
    return pltpu.with_memory_space_constraint(array, pltpu.VMEM)


def iota(shape, axis):
    return lax.broadcasted_iota(jnp.int32, shape, axis)


def edge_shape(field_edges, levels, lon):
    pieces = max(p for p in range(1, 8 // levels + 1) if lon // LANES % p == 0)
    return 8, field_edges // 8 * lon + lon // pieces


def write_edges(ref, edges, field_edges, levels):
    lon = edges.shape[1]
    groups = field_edges // 8
    for group in range(groups):
        part = edges[group * 8 : group * 8 + 8]
        ref[:, group * lon : (group + 1) * lon] = part.astype(jnp.bfloat16)
    width = ref.shape[1] - groups * lon
    courant = edges[field_edges : field_edges + levels]
    parts = [courant[:, at : at + width] for at in range(0, lon, width)]
    rest = 8 - len(parts) * levels
    if rest:
        parts.append(jnp.zeros((rest, width), jnp.float32))
    ref[:, groups * lon :] = jnp.concatenate(parts, axis=0).astype(jnp.bfloat16)


def read_edges(ref, field_edges, levels, lon):
    groups = field_edges // 8
    edges = ref[...].astype(jnp.float32)
    fields = [edges[:, group * lon : (group + 1) * lon] for group in range(groups)]
    width = edges.shape[1] - groups * lon
    courant = [
        edges[part * levels : (part + 1) * levels, groups * lon :] for part in range(lon // width)
    ]
    return fields, jnp.concatenate(courant, axis=1)


def write_stencil(stencil_ref, field_count, levels, rows):
    count = field_count * levels * rows
    speed_count = levels * rows
    lat = lax.axis_index("lat")
    lats = lax.axis_size("lat")
    odd = lat % 2

    own = (field_count + 1) * speed_count
    field_edges = field_count * levels * WIDTH
    column = iota((1, stencil_ref.shape[1]), 1)
    edge = column - own
    speed_edge = edge - 2 * field_edges
    is_own, is_speed = edge < 0, speed_edge >= 0
    far = jnp.where(is_speed, speed_edge // levels, edge // field_edges)
    field_edge = edge - far * field_edges
    edge_block = jnp.where(
        is_speed, speed_edge - far * levels + field_count * levels, field_edge // WIDTH
    )
    sides = jnp.where((lat > 0) & (lat < lats - 1), 2, 1)
    block = jnp.where(is_own, column // rows, jnp.where(far < sides, edge_block, -1))
    high = (odd + far + 1) % 2
    edge_place = jnp.where(is_speed, high * (rows + 1) - 1, field_edge % WIDTH - WIDTH + high * (rows + WIDTH))
    place = jnp.where(is_own, column % rows, edge_place)

    def relation(height, first_block):
        line = iota((height, 1), 0)
        line_block = line // rows
        row = line - line_block * rows
        return row, place - row, block == line_block + first_block

    def near_face(here, shift):
        return (here == shift) | (here == shift - 1)

    _, here, same = relation(count, 0)
    for side in range(2):
        outer = (here == side + 1) | (here == side - 2)
        value = jnp.where(near_face(here, side), 7.0, jnp.where(outer, -1.0, 0.0))
        stencil_ref[side * count : (side + 1) * count] = jnp.where(same, value, 0.0).astype(
            jnp.bfloat16
        )
    row, here, same = relation(speed_count, field_count * levels)
    live = ((row > 0) | (lat > 0), (row < rows - 1) | (lat < lats - 1))
    for side in range(2):
        first = 2 * count + side * speed_count
        value = jnp.where(same & near_face(here, side) & live[side], 0.5, 0.0)
        stencil_ref[first : first + speed_count] = value.astype(jnp.bfloat16)


def write_band_matrix(band_matrix_ref, polar_ref, mask_ref, band_ref, weight_ref, rows, levels):
    polar_row = iota(polar_ref.shape, 0)
    polar = jnp.zeros(polar_ref.shape, jnp.int32)
    for index in range(rows):
        polar = jnp.where(polar_row == index, mask_ref[:, index : index + 1], polar)
    polar_ref[...] = polar

    band_width, level_total = weight_ref.shape[1:]
    total = level_total * rows

    def level_at(index):
        place = index // rows
        position = place // levels
        return (member_at(position, level_total // levels) - position) * levels + place

    out_row, in_row = iota((total, 1), 0), iota((1, total), 1)
    of_row = level_at(out_row) == iota((1, level_total), 1)

    def spread(table):
        whole = jnp.concatenate([table] * level_total, axis=0)
        return jnp.sum(jnp.where(of_row, whole, jnp.zeros_like(whole)), axis=1, keepdims=True)

    start = spread(jnp.broadcast_to(band_ref[...], (rows, level_total)))
    offset = level_at(in_row) - start
    matrix = jnp.zeros((total, total), jnp.float32)
    for band in range(band_width):
        matrix = jnp.where(offset == band, spread(weight_ref[:, band, :]), matrix)
    matrix = jnp.where(in_row % rows == out_row % rows, matrix, 0.0)
    for part in range(PARTS):
        rounded = matrix.astype(jnp.bfloat16)
        band_matrix_ref[part * total : (part + 1) * total] = rounded
        matrix = matrix - rounded.astype(jnp.float32)


def edges_body(
    filter_hbm, fields_hbm, courant_hbm, mask_hbm, band_hbm, weight_hbm,
    near_ref, far_ref, stack_ref, stencil_ref, polar_ref, band_matrix_ref,
    mask_ref, band_ref, weight_ref, sems,
    *, field_count, levels, rows
):
    own = stack_ref.shape[0]
    blocks = own // rows
    field_rows = field_count * levels * rows
    pairs = (
        (weight_hbm, weight_ref),
        (band_hbm, band_ref),
        (mask_hbm, mask_ref),
        (fields_hbm, stack_ref.at[pl.ds(0, field_rows)]),
        (courant_hbm, stack_ref.at[pl.ds(field_rows, own - field_rows)]),
    )
    copies = [
        pltpu.make_async_copy(source, target, sems.at[index])
        for index, (source, target) in enumerate(pairs)
    ]
    for copy in copies:
        copy.start()
    odd = lax.axis_index("lat") % 2
    edge = iota((2 * EDGE_ROWS, 1), 0)
    far = (edge >= EDGE_ROWS).astype(jnp.int32)
    inner = edge - far * EDGE_ROWS
    high = (odd + far + 1) % 2
    field_edges = field_count * levels * WIDTH
    of_field = inner < field_edges
    block = jnp.where(of_field, inner // WIDTH, inner - field_edges + field_count * levels)
    row = jnp.where(of_field, inner % WIDTH + high * (rows - WIDTH), high * (rows - 1))
    wanted = jnp.where(block < blocks, block * rows + row, -1)
    pick = jnp.where(iota((2 * EDGE_ROWS, own), 1) == wanted, 1.0, 0.0).astype(jnp.bfloat16)
    write_stencil(stencil_ref, field_count, levels, rows)
    for copy in copies[:3]:
        copy.wait()
    write_band_matrix(band_matrix_ref, polar_ref, mask_ref, band_ref, weight_ref, rows, levels)
    for copy in copies[3:]:
        copy.wait()
    edges = jnp.dot(pick, stack_ref[...], preferred_element_type=jnp.float32)
    write_edges(near_ref, edges[:EDGE_ROWS], field_edges, levels)
    for member in range(2):
        write_edges(far_ref.at[member], edges[EDGE_ROWS:], field_edges, levels)


def tiles(field_count, levels, lon, units):
    for field in range(field_count):
        for part in range(lon // LANES):
            unit = field * (lon // LANES) + part
            for level in range(levels):
                yield field, level, part * LANES, (unit // units, unit % units, level)


def transport_body(
    near_ref, far_ref, stack_ref, stencil_ref, filter_ref, polar_ref, out_ref, *, field_count
):
    pieces, units, levels, rows, _ = out_ref.shape
    lon = stack_ref.shape[1]
    count = field_count * levels * rows
    speed_count = levels * rows
    field_edges = field_count * levels * WIDTH
    near_fields, near_courant = read_edges(near_ref, field_edges, levels, lon)
    partner = lax.axis_index("lat") % 2
    far_fields, far_courant = read_edges(far_ref.at[partner], field_edges, levels, lon)
    rest = EDGE_ROWS // 2 - 2 * levels
    speeds = [near_courant, far_courant, jnp.zeros((rest, lon), jnp.float32)]
    edges = jnp.concatenate(
        near_fields + far_fields + [jnp.concatenate(speeds, axis=0)], axis=0
    )
    source = jnp.concatenate([stack_ref[...], edges.astype(jnp.bfloat16)], axis=0)
    values = jnp.dot(stencil_ref[...], source, preferred_element_type=jnp.float32)
    speed_low = values[2 * count : 2 * count + speed_count] * (1.0 / 12.0)
    speed_high = values[2 * count + speed_count :] * (1.0 / 12.0)
    parts = []
    for first in range(0, count, speed_count):
        flux_low = speed_low * values[first : first + speed_count]
        flux_high = speed_high * values[count + first : count + first + speed_count]
        own = stack_ref[first : first + speed_count].astype(jnp.float32)
        parts.append(own - (flux_high - flux_low))
    moved = jnp.concatenate(parts, axis=0)

    def write(filtered):
        for field, level, at, place in tiles(field_count, levels, lon, units):
            first = (field * levels + level) * rows
            tile = filtered[first : first + rows, at : at + LANES]
            out_ref[place] = tile.astype(jnp.bfloat16)
        for unit in range(field_count * lon // LANES, pieces * units):
            out_ref[unit // units, unit % units] = jnp.zeros(out_ref.shape[2:], jnp.bfloat16)

    polar = polar_ref[...] == 1
    any_polar = jnp.max(polar_ref[...]) == 1

    @pl.when(any_polar)
    def _():
        correction = jnp.dot(
            moved.astype(jnp.bfloat16), filter_ref[...], preferred_element_type=jnp.float32
        )
        wide = jnp.concatenate([polar] * (lon // LANES), axis=1)
        whole = jnp.concatenate([wide] * (field_count * levels), axis=0)
        write(moved + jnp.where(whole, correction, 0.0))

    @pl.when(jnp.logical_not(any_polar))
    def _():
        write(moved)


def remap_body(band_matrix_ref, source_ref, out_ref):
    pieces, units, levels, rows, _ = source_ref.shape
    total = pieces * levels * rows
    columns = jnp.concatenate(
        [
            source_ref[:, unit].astype(jnp.float32).reshape(total, LANES).astype(jnp.bfloat16)
            for unit in range(units)
        ],
        axis=1,
    )
    split = jnp.dot(band_matrix_ref[...], columns, preferred_element_type=jnp.float32)
    result = split[(PARTS - 1) * total :]
    for part in range(PARTS - 1)[::-1]:
        result = result + split[part * total : (part + 1) * total]
    for unit in range(units):
        part = result[:, unit * LANES : (unit + 1) * LANES]
        out_ref[:, unit] = part.reshape(pieces, levels, rows, LANES).astype(jnp.bfloat16)


def collect_body(source_ref, out_hbm, out_ref, sems):
    field_count, levels, _, lon = out_ref.shape
    units = source_ref.shape[1]
    copies = []
    for field, level, at, place in tiles(field_count, levels, lon, units):
        out_ref[field, level, :, at : at + LANES] = source_ref[place]
        if at + LANES == lon and level == levels - 1:
            copy = pltpu.make_async_copy(out_ref.at[field], out_hbm.at[field], sems.at[field])
            copy.start()
            copies.append(copy)
    for copy in copies:
        copy.wait()


def on_device(fields, courant, filter_matrix, polar_mask, band_start, remap_weights):
    def array(*shape, dtype=jnp.bfloat16):
        return jax.ShapeDtypeStruct(shape, dtype)

    field_count, levels, rows, lon = fields.shape
    lats, levs = lax.axis_size("lat"), lax.axis_size("lev")
    level_total, band_width = remap_weights.shape[1:]
    if lon % LANES or rows % 8:
        raise ValueError("uneven tiles")
    units = -(-(field_count * lon // LANES) // levs)
    count = field_count * levels * rows
    blocks = (field_count + 1) * levels
    own = blocks * rows
    field_edges = field_count * levels * WIDTH
    if field_edges % 8 or 8 % levels or field_edges + levels > EDGE_ROWS:
        raise ValueError("uneven edges")
    edges = array(*edge_shape(field_edges, levels, lon))
    total = level_total * rows

    hbm = pl.BlockSpec(memory_space=pltpu.HBM)
    sizes = dict(field_count=field_count, levels=levels, rows=rows)
    small = [
        polar_mask.reshape(1, -1),
        band_start.reshape(1, -1),
        jnp.swapaxes(remap_weights, 1, 2),
    ]
    inputs = [filter_matrix, fields.reshape(count, lon), courant.reshape(own - count, lon), *small]
    near, far, stack, stencil, polar, band_matrix = pl.pallas_call(
        functools.partial(edges_body, **sizes),
        out_shape=(
            edges,
            array(2, *edges.shape),
            array(own, lon),
            array(2 * (count + levels * rows), own + 2 * field_edges + EDGE_ROWS // 2),
            array(rows, LANES, dtype=jnp.int32),
            array(PARTS * total, total),
        ),
        in_specs=[hbm] * len(inputs),
        out_specs=(WHOLE,) * 6,
        scratch_shapes=[pltpu.VMEM(each.shape, each.dtype) for each in small]
        + [pltpu.SemaphoreType.DMA((len(inputs) - 1,))],
        compiler_params=params(),
        cost_estimate=cost(2 * own * own * lon, 4 * own * lon),
    )(*map(in_hbm, inputs))

    near_pairs = [(i, i + 1) for i in range(0, lats - 1, 2)]
    from_near = lax.ppermute(
        near, "lat", near_pairs + [(target, source) for source, target in near_pairs]
    )
    far_groups = [[i, i + 1] for i in range(1, lats - 1, 2)] + [[0, lats - 1]]

    def exchange_far(array):
        return lax.all_to_all(
            array, "lat", split_axis=0, concat_axis=0, tiled=True, axis_index_groups=far_groups
        )

    lat_index = lax.axis_index("lat")
    has_far = (lat_index > 0) & (lat_index < lats - 1)
    from_far = lax.cond(has_far, exchange_far, lambda array: array, far)

    pieces = pl.pallas_call(
        functools.partial(transport_body, field_count=field_count),
        out_shape=array(levs, units, levels, rows, LANES),
        in_specs=[WHOLE] * 6,
        out_specs=WHOLE,
        compiler_params=params(),
        cost_estimate=cost(2 * count * lon * lon, 2 * lon * lon),
    )(from_near, from_far, stack, stencil, in_vmem(filter_matrix), polar)

    def exchange(array):
        group = exchange_order(levs)
        return lax.all_to_all(
            array, "lev", split_axis=0, concat_axis=0, tiled=True, axis_index_groups=[group]
        )

    remapped = pl.pallas_call(
        remap_body,
        out_shape=array(*pieces.shape),
        in_specs=[WHOLE] * 2,
        out_specs=WHOLE,
        compiler_params=params(),
        cost_estimate=cost(6 * total * total * units * LANES, 4 * total * units * LANES),
    )(band_matrix, exchange(pieces))
    return pl.pallas_call(
        collect_body,
        out_shape=array(*fields.shape),
        in_specs=[WHOLE],
        out_specs=hbm,
        scratch_shapes=[
            pltpu.VMEM(fields.shape, fields.dtype),
            pltpu.SemaphoreType.DMA((field_count,)),
        ],
        compiler_params=params(),
        cost_estimate=cost(count * lon, 4 * count * lon),
    )(exchange(remapped))


def solution(mesh):
    return jax.shard_map(
        on_device,
        mesh=mesh,
        in_specs=(
            P(None, "lev", "lat", None),
            P("lev", "lat", None),
            P(),
            P("lat"),
            P(),
            P("lat", None, None),
        ),
        out_specs=P(None, "lev", "lat", None),
        check_vma=False,
    )
```

```python
import functools

import jax
import jax.numpy as jnp
from jax import lax
from jax.experimental import pallas as pl
from jax.experimental.pallas import tpu as pltpu
from jax.sharding import PartitionSpec as P

WIDTH = 2
LANES = 128
EDGE_ROWS = 32
PARTS = 2
VMEM_LIMIT = 48 * 1024 * 1024
WHOLE = pl.BlockSpec(memory_space=pltpu.VMEM)


def cost(flops, moved):
    return pl.CostEstimate(flops=flops, bytes_accessed=moved, transcendentals=0)


def params():
    return pltpu.CompilerParams(vmem_limit_bytes=VMEM_LIMIT)


def exchange_order(count):
    order = list(range(count))[::-1]
    return order[3:] + order[:3]


def member_at(position, count):
    member = jnp.zeros_like(position)
    for place, index in enumerate(exchange_order(count)):
        member = jnp.where(position == place, index, member)
    return member


def in_hbm(array):
    return pltpu.with_memory_space_constraint(array, pltpu.HBM)


def in_vmem(array):
    return pltpu.with_memory_space_constraint(array, pltpu.VMEM)


def iota(shape, axis):
    return lax.broadcasted_iota(jnp.int32, shape, axis)


def edge_shape(field_edges, levels, lon):
    pieces = max(p for p in range(1, 8 // levels + 1) if lon // LANES % p == 0)
    return 8, field_edges // 8 * lon + lon // pieces


def write_edges(ref, edges, field_edges, levels):
    lon = edges.shape[1]
    groups = field_edges // 8
    for group in range(groups):
        part = edges[group * 8 : group * 8 + 8]
        ref[:, group * lon : (group + 1) * lon] = part.astype(jnp.bfloat16)
    width = ref.shape[1] - groups * lon
    courant = edges[field_edges : field_edges + levels]
    parts = [courant[:, at : at + width] for at in range(0, lon, width)]
    rest = 8 - len(parts) * levels
    if rest:
        parts.append(jnp.zeros((rest, width), jnp.float32))
    ref[:, groups * lon :] = jnp.concatenate(parts, axis=0).astype(jnp.bfloat16)


def read_edges(ref, field_edges, levels, lon):
    groups = field_edges // 8
    edges = ref[...].astype(jnp.float32)
    fields = [edges[:, group * lon : (group + 1) * lon] for group in range(groups)]
    width = edges.shape[1] - groups * lon
    courant = [
        edges[part * levels : (part + 1) * levels, groups * lon :] for part in range(lon // width)
    ]
    return fields, jnp.concatenate(courant, axis=1)


def write_stencil(stencil_ref, field_count, levels, rows):
    count = field_count * levels * rows
    speed_count = levels * rows
    lat = lax.axis_index("lat")
    lats = lax.axis_size("lat")
    odd = lat % 2

    own = (field_count + 1) * speed_count
    field_edges = field_count * levels * WIDTH
    column = iota((1, stencil_ref.shape[1]), 1)
    edge = column - own
    speed_edge = edge - 2 * field_edges
    is_own, is_speed = edge < 0, speed_edge >= 0
    far = jnp.where(is_speed, speed_edge // levels, edge // field_edges)
    field_edge = edge - far * field_edges
    edge_block = jnp.where(
        is_speed, speed_edge - far * levels + field_count * levels, field_edge // WIDTH
    )
    sides = jnp.where((lat > 0) & (lat < lats - 1), 2, 1)
    block = jnp.where(is_own, column // rows, jnp.where(far < sides, edge_block, -1))
    high = (odd + far + 1) % 2
    edge_place = jnp.where(is_speed, high * (rows + 1) - 1, field_edge % WIDTH - WIDTH + high * (rows + WIDTH))
    place = jnp.where(is_own, column % rows, edge_place)

    def relation(height, first_block):
        line = iota((height, 1), 0)
        line_block = line // rows
        row = line - line_block * rows
        return row, place - row, block == line_block + first_block

    def near_face(here, shift):
        return (here == shift) | (here == shift - 1)

    _, here, same = relation(count, 0)
    for side in range(2):
        outer = (here == side + 1) | (here == side - 2)
        value = jnp.where(near_face(here, side), 7.0, jnp.where(outer, -1.0, 0.0))
        stencil_ref[side * count : (side + 1) * count] = jnp.where(same, value, 0.0).astype(
            jnp.bfloat16
        )
    row, here, same = relation(speed_count, field_count * levels)
    live = ((row > 0) | (lat > 0), (row < rows - 1) | (lat < lats - 1))
    for side in range(2):
        first = 2 * count + side * speed_count
        value = jnp.where(same & near_face(here, side) & live[side], 0.5, 0.0)
        stencil_ref[first : first + speed_count] = value.astype(jnp.bfloat16)


def write_band_matrix(band_matrix_ref, polar_ref, mask_ref, band_ref, weight_ref, rows, levels):
    polar_row = iota(polar_ref.shape, 0)
    polar = jnp.zeros(polar_ref.shape, jnp.int32)
    for index in range(rows):
        polar = jnp.where(polar_row == index, mask_ref[:, index : index + 1], polar)
    polar_ref[...] = polar

    band_width, level_total = weight_ref.shape[1:]
    total = level_total * rows

    def level_at(index):
        place = index // rows
        position = place // levels
        return (member_at(position, level_total // levels) - position) * levels + place

    out_row, in_row = iota((total, 1), 0), iota((1, total), 1)
    of_row = level_at(out_row) == iota((1, level_total), 1)

    def spread(table):
        whole = jnp.concatenate([table] * level_total, axis=0)
        return jnp.sum(jnp.where(of_row, whole, jnp.zeros_like(whole)), axis=1, keepdims=True)

    start = spread(jnp.broadcast_to(band_ref[...], (rows, level_total)))
    offset = level_at(in_row) - start
    matrix = jnp.zeros((total, total), jnp.float32)
    for band in range(band_width):
        matrix = jnp.where(offset == band, spread(weight_ref[:, band, :]), matrix)
    matrix = jnp.where(in_row % rows == out_row % rows, matrix, 0.0)
    for part in range(PARTS):
        rounded = matrix.astype(jnp.bfloat16)
        band_matrix_ref[part * total : (part + 1) * total] = rounded
        matrix = matrix - rounded.astype(jnp.float32)


def edges_body(
    filter_hbm, fields_hbm, courant_hbm, mask_hbm, band_hbm, weight_hbm,
    near_ref, far_ref, stack_ref, stencil_ref, polar_ref, band_matrix_ref,
    mask_ref, band_ref, weight_ref, sems,
    *, field_count, levels, rows
):
    own = stack_ref.shape[0]
    blocks = own // rows
    field_rows = field_count * levels * rows
    pairs = (
        (weight_hbm, weight_ref),
        (band_hbm, band_ref),
        (mask_hbm, mask_ref),
        (fields_hbm, stack_ref.at[pl.ds(0, field_rows)]),
        (courant_hbm, stack_ref.at[pl.ds(field_rows, own - field_rows)]),
    )
    copies = [
        pltpu.make_async_copy(source, target, sems.at[index])
        for index, (source, target) in enumerate(pairs)
    ]
    for copy in copies:
        copy.start()
    odd = lax.axis_index("lat") % 2
    edge = iota((2 * EDGE_ROWS, 1), 0)
    far = (edge >= EDGE_ROWS).astype(jnp.int32)
    inner = edge - far * EDGE_ROWS
    high = (odd + far + 1) % 2
    field_edges = field_count * levels * WIDTH
    of_field = inner < field_edges
    block = jnp.where(of_field, inner // WIDTH, inner - field_edges + field_count * levels)
    row = jnp.where(of_field, inner % WIDTH + high * (rows - WIDTH), high * (rows - 1))
    wanted = jnp.where(block < blocks, block * rows + row, -1)
    pick = jnp.where(iota((2 * EDGE_ROWS, own), 1) == wanted, 1.0, 0.0).astype(jnp.bfloat16)
    write_stencil(stencil_ref, field_count, levels, rows)
    for copy in copies[:3]:
        copy.wait()
    write_band_matrix(band_matrix_ref, polar_ref, mask_ref, band_ref, weight_ref, rows, levels)
    for copy in copies[3:]:
        copy.wait()
    edges = jnp.dot(pick, stack_ref[...], preferred_element_type=jnp.float32)
    write_edges(near_ref, edges[:EDGE_ROWS], field_edges, levels)
    for member in range(2):
        write_edges(far_ref.at[member], edges[EDGE_ROWS:], field_edges, levels)


def tiles(field_count, levels, lon, units):
    for field in range(field_count):
        for part in range(lon // LANES):
            unit = field * (lon // LANES) + part
            for level in range(levels):
                yield field, level, part * LANES, (unit // units, unit % units, level)


def transport_body(
    near_ref, far_ref, stack_ref, stencil_ref, filter_ref, polar_ref, out_ref, *, field_count
):
    pieces, units, levels, rows, _ = out_ref.shape
    lon = stack_ref.shape[1]
    count = field_count * levels * rows
    speed_count = levels * rows
    field_edges = field_count * levels * WIDTH
    near_fields, near_courant = read_edges(near_ref, field_edges, levels, lon)
    partner = lax.axis_index("lat") % 2
    far_fields, far_courant = read_edges(far_ref.at[partner], field_edges, levels, lon)
    rest = EDGE_ROWS // 2 - 2 * levels
    speeds = [near_courant, far_courant, jnp.zeros((rest, lon), jnp.float32)]
    edges = jnp.concatenate(
        near_fields + far_fields + [jnp.concatenate(speeds, axis=0)], axis=0
    )
    source = jnp.concatenate([stack_ref[...], edges.astype(jnp.bfloat16)], axis=0)
    values = jnp.dot(stencil_ref[...], source, preferred_element_type=jnp.float32)
    speed_low = values[2 * count : 2 * count + speed_count] * (1.0 / 12.0)
    speed_high = values[2 * count + speed_count :] * (1.0 / 12.0)
    parts = []
    for first in range(0, count, speed_count):
        flux_low = speed_low * values[first : first + speed_count]
        flux_high = speed_high * values[count + first : count + first + speed_count]
        own = stack_ref[first : first + speed_count].astype(jnp.float32)
        parts.append(own - (flux_high - flux_low))
    moved = jnp.concatenate(parts, axis=0)

    def write(filtered):
        for field, level, at, place in tiles(field_count, levels, lon, units):
            first = (field * levels + level) * rows
            tile = filtered[first : first + rows, at : at + LANES]
            out_ref[place] = tile.astype(jnp.bfloat16)
        for unit in range(field_count * lon // LANES, pieces * units):
            out_ref[unit // units, unit % units] = jnp.zeros(out_ref.shape[2:], jnp.bfloat16)

    polar = polar_ref[...] == 1
    any_polar = jnp.max(polar_ref[...]) == 1

    @pl.when(any_polar)
    def _():
        correction = jnp.dot(
            moved.astype(jnp.bfloat16), filter_ref[...], preferred_element_type=jnp.float32
        )
        wide = jnp.concatenate([polar] * (lon // LANES), axis=1)
        whole = jnp.concatenate([wide] * (field_count * levels), axis=0)
        write(moved + jnp.where(whole, correction, 0.0))

    @pl.when(jnp.logical_not(any_polar))
    def _():
        write(moved)


def remap_body(band_matrix_ref, source_ref, out_ref):
    pieces, units, levels, rows, _ = source_ref.shape
    total = pieces * levels * rows
    columns = jnp.concatenate(
        [
            source_ref[:, unit].astype(jnp.float32).reshape(total, LANES).astype(jnp.bfloat16)
            for unit in range(units)
        ],
        axis=1,
    )
    split = jnp.dot(band_matrix_ref[...], columns, preferred_element_type=jnp.float32)
    result = split[(PARTS - 1) * total :]
    for part in range(PARTS - 1)[::-1]:
        result = result + split[part * total : (part + 1) * total]
    for unit in range(units):
        part = result[:, unit * LANES : (unit + 1) * LANES]
        out_ref[:, unit] = part.reshape(pieces, levels, rows, LANES).astype(jnp.bfloat16)


def collect_body(source_ref, out_hbm, out_ref, sems):
    field_count, levels, _, lon = out_ref.shape
    units = source_ref.shape[1]
    copies = []
    for field, level, at, place in tiles(field_count, levels, lon, units):
        out_ref[field, level, :, at : at + LANES] = source_ref[place]
        if at + LANES == lon and level == levels - 1:
            copy = pltpu.make_async_copy(out_ref.at[field], out_hbm.at[field], sems.at[field])
            copy.start()
            copies.append(copy)
    for copy in copies:
        copy.wait()


def on_device(fields, courant, filter_matrix, polar_mask, band_start, remap_weights):
    def array(*shape, dtype=jnp.bfloat16):
        return jax.ShapeDtypeStruct(shape, dtype)

    field_count, levels, rows, lon = fields.shape
    lats, levs = lax.axis_size("lat"), lax.axis_size("lev")
    level_total, band_width = remap_weights.shape[1:]
    if lon % LANES or rows % 8:
        raise ValueError("uneven tiles")
    units = -(-(field_count * lon // LANES) // levs)
    count = field_count * levels * rows
    blocks = (field_count + 1) * levels
    own = blocks * rows
    field_edges = field_count * levels * WIDTH
    if field_edges % 8 or 8 % levels or field_edges + levels > EDGE_ROWS:
        raise ValueError("uneven edges")
    edges = array(*edge_shape(field_edges, levels, lon))
    total = level_total * rows

    hbm = pl.BlockSpec(memory_space=pltpu.HBM)
    sizes = dict(field_count=field_count, levels=levels, rows=rows)
    small = [
        polar_mask.reshape(1, -1),
        band_start.reshape(1, -1),
        jnp.swapaxes(remap_weights, 1, 2),
    ]
    inputs = [filter_matrix, fields.reshape(count, lon), courant.reshape(own - count, lon), *small]
    near, far, stack, stencil, polar, band_matrix = pl.pallas_call(
        functools.partial(edges_body, **sizes),
        out_shape=(
            edges,
            array(2, *edges.shape),
            array(own, lon),
            array(2 * (count + levels * rows), own + 2 * field_edges + EDGE_ROWS // 2),
            array(rows, LANES, dtype=jnp.int32),
            array(PARTS * total, total),
        ),
        in_specs=[hbm] * len(inputs),
        out_specs=(WHOLE,) * 6,
        scratch_shapes=[pltpu.VMEM(each.shape, each.dtype) for each in small]
        + [pltpu.SemaphoreType.DMA((len(inputs) - 1,))],
        compiler_params=params(),
        cost_estimate=cost(2 * own * own * lon, 4 * own * lon),
    )(*map(in_hbm, inputs))

    near_pairs = [(i, i + 1) for i in range(0, lats - 1, 2)]
    from_near = lax.ppermute(
        near, "lat", near_pairs + [(target, source) for source, target in near_pairs]
    )
    far_groups = [[i, i + 1] for i in range(1, lats - 1, 2)] + [[0, lats - 1]]

    def exchange_far(array):
        return lax.all_to_all(
            array, "lat", split_axis=0, concat_axis=0, tiled=True, axis_index_groups=far_groups
        )

    lat_index = lax.axis_index("lat")
    has_far = (lat_index > 0) & (lat_index < lats - 1)
    from_far = lax.cond(has_far, exchange_far, lambda array: array, far)

    pieces = pl.pallas_call(
        functools.partial(transport_body, field_count=field_count),
        out_shape=array(levs, units, levels, rows, LANES),
        in_specs=[WHOLE] * 6,
        out_specs=WHOLE,
        compiler_params=params(),
        cost_estimate=cost(2 * count * lon * lon, 2 * lon * lon),
    )(from_near, from_far, stack, stencil, in_vmem(filter_matrix), polar)

    def exchange(array):
        group = exchange_order(levs)
        return lax.all_to_all(
            array, "lev", split_axis=0, concat_axis=0, tiled=True, axis_index_groups=[group]
        )

    remapped = pl.pallas_call(
        remap_body,
        out_shape=array(*pieces.shape),
        in_specs=[WHOLE] * 2,
        out_specs=WHOLE,
        compiler_params=params(),
        cost_estimate=cost(6 * total * total * units * LANES, 4 * total * units * LANES),
    )(band_matrix, exchange(pieces))
    return pl.pallas_call(
        collect_body,
        out_shape=array(*fields.shape),
        in_specs=[WHOLE],
        out_specs=hbm,
        scratch_shapes=[
            pltpu.VMEM(fields.shape, fields.dtype),
            pltpu.SemaphoreType.DMA((field_count,)),
        ],
        compiler_params=params(),
        cost_estimate=cost(count * lon, 4 * count * lon),
    )(exchange(remapped))


def solution(mesh):
    return jax.shard_map(
        on_device,
        mesh=mesh,
        in_specs=(
            P(None, "lev", "lat", None),
            P("lev", "lat", None),
            P(),
            P("lat"),
            P(),
            P("lat", None, None),
        ),
        out_specs=P(None, "lev", "lat", None),
        check_vma=False,
    )
```

```python
import functools

import jax
import jax.numpy as jnp
from jax import lax
from jax.experimental import pallas as pl
from jax.experimental.pallas import tpu as pltpu
from jax.sharding import PartitionSpec as P

WIDTH = 2
LANES = 128
EDGE_ROWS = 32
PARTS = 2
VMEM_LIMIT = 48 * 1024 * 1024
WHOLE = pl.BlockSpec(memory_space=pltpu.VMEM)


def cost(flops, moved):
    return pl.CostEstimate(flops=flops, bytes_accessed=moved, transcendentals=0)


def params():
    return pltpu.CompilerParams(vmem_limit_bytes=VMEM_LIMIT)


def exchange_order(count):
    order = [index ^ (index // 2 % 2 == 1) for index in range(count)][::-1]
    return order[2:] + order[:2]


def member_at(position, count):
    member = jnp.zeros_like(position)
    for place, index in enumerate(exchange_order(count)):
        member = jnp.where(position == place, index, member)
    return member


def in_hbm(array):
    return pltpu.with_memory_space_constraint(array, pltpu.HBM)


def in_vmem(array):
    return pltpu.with_memory_space_constraint(array, pltpu.VMEM)


def iota(shape, axis):
    return lax.broadcasted_iota(jnp.int32, shape, axis)


def edge_shape(field_edges, levels, lon):
    pieces = max(p for p in range(1, 8 // levels + 1) if lon // LANES % p == 0)
    return 8, field_edges // 8 * lon + lon // pieces


def write_edges(ref, edges, field_edges, levels):
    lon = edges.shape[1]
    groups = field_edges // 8
    for group in range(groups):
        part = edges[group * 8 : group * 8 + 8]
        ref[:, group * lon : (group + 1) * lon] = part.astype(jnp.bfloat16)
    width = ref.shape[1] - groups * lon
    courant = edges[field_edges : field_edges + levels]
    parts = [courant[:, at : at + width] for at in range(0, lon, width)]
    rest = 8 - len(parts) * levels
    if rest:
        parts.append(jnp.zeros((rest, width), jnp.float32))
    ref[:, groups * lon :] = jnp.concatenate(parts, axis=0).astype(jnp.bfloat16)


def read_edges(ref, field_edges, levels, lon):
    groups = field_edges // 8
    edges = ref[...].astype(jnp.float32)
    fields = [edges[:, group * lon : (group + 1) * lon] for group in range(groups)]
    width = edges.shape[1] - groups * lon
    courant = [
        edges[part * levels : (part + 1) * levels, groups * lon :] for part in range(lon // width)
    ]
    return fields, jnp.concatenate(courant, axis=1)


def write_stencil(stencil_ref, field_count, levels, rows):
    count = field_count * levels * rows
    speed_count = levels * rows
    lat = lax.axis_index("lat")
    lats = lax.axis_size("lat")
    odd = lat % 2

    own = (field_count + 1) * speed_count
    field_edges = field_count * levels * WIDTH
    column = iota((1, stencil_ref.shape[1]), 1)
    edge = column - own
    speed_edge = edge - 2 * field_edges
    is_own, is_speed = edge < 0, speed_edge >= 0
    far = jnp.where(is_speed, speed_edge // levels, edge // field_edges)
    field_edge = edge - far * field_edges
    edge_block = jnp.where(
        is_speed, speed_edge - far * levels + field_count * levels, field_edge // WIDTH
    )
    sides = jnp.where((lat > 0) & (lat < lats - 1), 2, 1)
    block = jnp.where(is_own, column // rows, jnp.where(far < sides, edge_block, -1))
    high = (odd + far + 1) % 2
    edge_place = jnp.where(is_speed, high * (rows + 1) - 1, field_edge % WIDTH - WIDTH + high * (rows + WIDTH))
    place = jnp.where(is_own, column % rows, edge_place)

    def relation(height, first_block):
        line = iota((height, 1), 0)
        line_block = line // rows
        row = line - line_block * rows
        return row, place - row, block == line_block + first_block

    def near_face(here, shift):
        return (here == shift) | (here == shift - 1)

    _, here, same = relation(count, 0)
    for side in range(2):
        outer = (here == side + 1) | (here == side - 2)
        value = jnp.where(near_face(here, side), 7.0, jnp.where(outer, -1.0, 0.0))
        stencil_ref[side * count : (side + 1) * count] = jnp.where(same, value, 0.0).astype(
            jnp.bfloat16
        )
    row, here, same = relation(speed_count, field_count * levels)
    live = ((row > 0) | (lat > 0), (row < rows - 1) | (lat < lats - 1))
    for side in range(2):
        first = 2 * count + side * speed_count
        value = jnp.where(same & near_face(here, side) & live[side], 0.5, 0.0)
        stencil_ref[first : first + speed_count] = value.astype(jnp.bfloat16)


def write_band_matrix(band_matrix_ref, polar_ref, mask_ref, band_ref, weight_ref, rows, levels):
    polar_row = iota(polar_ref.shape, 0)
    polar = jnp.zeros(polar_ref.shape, jnp.int32)
    for index in range(rows):
        polar = jnp.where(polar_row == index, mask_ref[:, index : index + 1], polar)
    polar_ref[...] = polar

    band_width, level_total = weight_ref.shape[1:]
    total = level_total * rows

    def level_at(index):
        place = index // rows
        position = place // levels
        return (member_at(position, level_total // levels) - position) * levels + place

    out_row, in_row = iota((total, 1), 0), iota((1, total), 1)
    of_row = level_at(out_row) == iota((1, level_total), 1)

    def spread(table):
        whole = jnp.concatenate([table] * level_total, axis=0)
        return jnp.sum(jnp.where(of_row, whole, jnp.zeros_like(whole)), axis=1, keepdims=True)

    start = spread(jnp.broadcast_to(band_ref[...], (rows, level_total)))
    offset = level_at(in_row) - start
    matrix = jnp.zeros((total, total), jnp.float32)
    for band in range(band_width):
        matrix = jnp.where(offset == band, spread(weight_ref[:, band, :]), matrix)
    matrix = jnp.where(in_row % rows == out_row % rows, matrix, 0.0)
    for part in range(PARTS):
        rounded = matrix.astype(jnp.bfloat16)
        band_matrix_ref[part * total : (part + 1) * total] = rounded
        matrix = matrix - rounded.astype(jnp.float32)


def edges_body(
    filter_hbm, fields_hbm, courant_hbm, mask_hbm, band_hbm, weight_hbm,
    near_ref, far_ref, stack_ref, stencil_ref, polar_ref, band_matrix_ref,
    mask_ref, band_ref, weight_ref, sems,
    *, field_count, levels, rows
):
    own = stack_ref.shape[0]
    blocks = own // rows
    field_rows = field_count * levels * rows
    pairs = (
        (weight_hbm, weight_ref),
        (band_hbm, band_ref),
        (mask_hbm, mask_ref),
        (fields_hbm, stack_ref.at[pl.ds(0, field_rows)]),
        (courant_hbm, stack_ref.at[pl.ds(field_rows, own - field_rows)]),
    )
    copies = [
        pltpu.make_async_copy(source, target, sems.at[index])
        for index, (source, target) in enumerate(pairs)
    ]
    for copy in copies:
        copy.start()
    odd = lax.axis_index("lat") % 2
    edge = iota((2 * EDGE_ROWS, 1), 0)
    far = (edge >= EDGE_ROWS).astype(jnp.int32)
    inner = edge - far * EDGE_ROWS
    high = (odd + far + 1) % 2
    field_edges = field_count * levels * WIDTH
    of_field = inner < field_edges
    block = jnp.where(of_field, inner // WIDTH, inner - field_edges + field_count * levels)
    row = jnp.where(of_field, inner % WIDTH + high * (rows - WIDTH), high * (rows - 1))
    wanted = jnp.where(block < blocks, block * rows + row, -1)
    pick = jnp.where(iota((2 * EDGE_ROWS, own), 1) == wanted, 1.0, 0.0).astype(jnp.bfloat16)
    write_stencil(stencil_ref, field_count, levels, rows)
    for copy in copies[:3]:
        copy.wait()
    write_band_matrix(band_matrix_ref, polar_ref, mask_ref, band_ref, weight_ref, rows, levels)
    for copy in copies[3:]:
        copy.wait()
    edges = jnp.dot(pick, stack_ref[...], preferred_element_type=jnp.float32)
    write_edges(near_ref, edges[:EDGE_ROWS], field_edges, levels)
    for member in range(2):
        write_edges(far_ref.at[member], edges[EDGE_ROWS:], field_edges, levels)


def tiles(field_count, levels, lon, units):
    for field in range(field_count):
        for part in range(lon // LANES):
            unit = field * (lon // LANES) + part
            for level in range(levels):
                yield field, level, part * LANES, (unit // units, unit % units, level)


def transport_body(
    near_ref, far_ref, stack_ref, stencil_ref, filter_ref, polar_ref, out_ref, *, field_count
):
    pieces, units, levels, rows, _ = out_ref.shape
    lon = stack_ref.shape[1]
    count = field_count * levels * rows
    speed_count = levels * rows
    field_edges = field_count * levels * WIDTH
    near_fields, near_courant = read_edges(near_ref, field_edges, levels, lon)
    partner = lax.axis_index("lat") % 2
    far_fields, far_courant = read_edges(far_ref.at[partner], field_edges, levels, lon)
    rest = EDGE_ROWS // 2 - 2 * levels
    speeds = [near_courant, far_courant, jnp.zeros((rest, lon), jnp.float32)]
    edges = jnp.concatenate(
        near_fields + far_fields + [jnp.concatenate(speeds, axis=0)], axis=0
    )
    source = jnp.concatenate([stack_ref[...], edges.astype(jnp.bfloat16)], axis=0)
    values = jnp.dot(stencil_ref[...], source, preferred_element_type=jnp.float32)
    speed_low = values[2 * count : 2 * count + speed_count] * (1.0 / 12.0)
    speed_high = values[2 * count + speed_count :] * (1.0 / 12.0)
    parts = []
    for first in range(0, count, speed_count):
        flux_low = speed_low * values[first : first + speed_count]
        flux_high = speed_high * values[count + first : count + first + speed_count]
        own = stack_ref[first : first + speed_count].astype(jnp.float32)
        parts.append(own - (flux_high - flux_low))
    moved = jnp.concatenate(parts, axis=0)

    def write(filtered):
        for field, level, at, place in tiles(field_count, levels, lon, units):
            first = (field * levels + level) * rows
            tile = filtered[first : first + rows, at : at + LANES]
            out_ref[place] = tile.astype(jnp.bfloat16)
        for unit in range(field_count * lon // LANES, pieces * units):
            out_ref[unit // units, unit % units] = jnp.zeros(out_ref.shape[2:], jnp.bfloat16)

    polar = polar_ref[...] == 1
    any_polar = jnp.max(polar_ref[...]) == 1

    @pl.when(any_polar)
    def _():
        correction = jnp.dot(
            moved.astype(jnp.bfloat16), filter_ref[...], preferred_element_type=jnp.float32
        )
        wide = jnp.concatenate([polar] * (lon // LANES), axis=1)
        whole = jnp.concatenate([wide] * (field_count * levels), axis=0)
        write(moved + jnp.where(whole, correction, 0.0))

    @pl.when(jnp.logical_not(any_polar))
    def _():
        write(moved)


def remap_body(band_matrix_ref, source_ref, out_ref):
    pieces, units, levels, rows, _ = source_ref.shape
    total = pieces * levels * rows
    columns = jnp.concatenate(
        [
            source_ref[:, unit].astype(jnp.float32).reshape(total, LANES).astype(jnp.bfloat16)
            for unit in range(units)
        ],
        axis=1,
    )
    split = jnp.dot(band_matrix_ref[...], columns, preferred_element_type=jnp.float32)
    result = split[(PARTS - 1) * total :]
    for part in range(PARTS - 1)[::-1]:
        result = result + split[part * total : (part + 1) * total]
    for unit in range(units):
        part = result[:, unit * LANES : (unit + 1) * LANES]
        out_ref[:, unit] = part.reshape(pieces, levels, rows, LANES).astype(jnp.bfloat16)


def collect_body(source_ref, out_hbm, out_ref, sems):
    field_count, levels, _, lon = out_ref.shape
    units = source_ref.shape[1]
    copies = []
    for field, level, at, place in tiles(field_count, levels, lon, units):
        out_ref[field, level, :, at : at + LANES] = source_ref[place]
        if at + LANES == lon and level == levels - 1:
            copy = pltpu.make_async_copy(out_ref.at[field], out_hbm.at[field], sems.at[field])
            copy.start()
            copies.append(copy)
    for copy in copies:
        copy.wait()


def on_device(fields, courant, filter_matrix, polar_mask, band_start, remap_weights):
    def array(*shape, dtype=jnp.bfloat16):
        return jax.ShapeDtypeStruct(shape, dtype)

    field_count, levels, rows, lon = fields.shape
    lats, levs = lax.axis_size("lat"), lax.axis_size("lev")
    level_total, band_width = remap_weights.shape[1:]
    if lon % LANES or rows % 8:
        raise ValueError("uneven tiles")
    units = -(-(field_count * lon // LANES) // levs)
    count = field_count * levels * rows
    blocks = (field_count + 1) * levels
    own = blocks * rows
    field_edges = field_count * levels * WIDTH
    if field_edges % 8 or 8 % levels or field_edges + levels > EDGE_ROWS:
        raise ValueError("uneven edges")
    edges = array(*edge_shape(field_edges, levels, lon))
    total = level_total * rows

    hbm = pl.BlockSpec(memory_space=pltpu.HBM)
    sizes = dict(field_count=field_count, levels=levels, rows=rows)
    small = [
        polar_mask.reshape(1, -1),
        band_start.reshape(1, -1),
        jnp.swapaxes(remap_weights, 1, 2),
    ]
    inputs = [filter_matrix, fields.reshape(count, lon), courant.reshape(own - count, lon), *small]
    near, far, stack, stencil, polar, band_matrix = pl.pallas_call(
        functools.partial(edges_body, **sizes),
        out_shape=(
            edges,
            array(2, *edges.shape),
            array(own, lon),
            array(2 * (count + levels * rows), own + 2 * field_edges + EDGE_ROWS // 2),
            array(rows, LANES, dtype=jnp.int32),
            array(PARTS * total, total),
        ),
        in_specs=[hbm] * len(inputs),
        out_specs=(WHOLE,) * 6,
        scratch_shapes=[pltpu.VMEM(each.shape, each.dtype) for each in small]
        + [pltpu.SemaphoreType.DMA((len(inputs) - 1,))],
        compiler_params=params(),
        cost_estimate=cost(2 * own * own * lon, 4 * own * lon),
    )(*map(in_hbm, inputs))

    near_pairs = [(i, i + 1) for i in range(0, lats - 1, 2)]
    from_near = lax.ppermute(
        near, "lat", near_pairs + [(target, source) for source, target in near_pairs]
    )
    far_groups = [[i, i + 1] for i in range(1, lats - 1, 2)] + [[0, lats - 1]]

    def exchange_far(array):
        return lax.all_to_all(
            array, "lat", split_axis=0, concat_axis=0, tiled=True, axis_index_groups=far_groups
        )

    lat_index = lax.axis_index("lat")
    has_far = (lat_index > 0) & (lat_index < lats - 1)
    from_far = lax.cond(has_far, exchange_far, lambda array: array, far)

    pieces = pl.pallas_call(
        functools.partial(transport_body, field_count=field_count),
        out_shape=array(levs, units, levels, rows, LANES),
        in_specs=[WHOLE] * 6,
        out_specs=WHOLE,
        compiler_params=params(),
        cost_estimate=cost(2 * count * lon * lon, 2 * lon * lon),
    )(from_near, from_far, stack, stencil, in_vmem(filter_matrix), polar)

    def exchange(array):
        group = exchange_order(levs)
        return lax.all_to_all(
            array, "lev", split_axis=0, concat_axis=0, tiled=True, axis_index_groups=[group]
        )

    remapped = pl.pallas_call(
        remap_body,
        out_shape=array(*pieces.shape),
        in_specs=[WHOLE] * 2,
        out_specs=WHOLE,
        compiler_params=params(),
        cost_estimate=cost(6 * total * total * units * LANES, 4 * total * units * LANES),
    )(band_matrix, exchange(pieces))
    return pl.pallas_call(
        collect_body,
        out_shape=array(*fields.shape),
        in_specs=[WHOLE],
        out_specs=hbm,
        scratch_shapes=[
            pltpu.VMEM(fields.shape, fields.dtype),
            pltpu.SemaphoreType.DMA((field_count,)),
        ],
        compiler_params=params(),
        cost_estimate=cost(count * lon, 4 * count * lon),
    )(exchange(remapped))


def solution(mesh):
    return jax.shard_map(
        on_device,
        mesh=mesh,
        in_specs=(
            P(None, "lev", "lat", None),
            P("lev", "lat", None),
            P(),
            P("lat"),
            P(),
            P("lat", None, None),
        ),
        out_specs=P(None, "lev", "lat", None),
        check_vma=False,
    )
```

```python
import functools

import jax
import jax.numpy as jnp
from jax import lax
from jax.experimental import pallas as pl
from jax.experimental.pallas import tpu as pltpu
from jax.sharding import PartitionSpec as P

WIDTH = 2
LANES = 128
EDGE_ROWS = 32
PARTS = 2
VMEM_LIMIT = 48 * 1024 * 1024
WHOLE = pl.BlockSpec(memory_space=pltpu.VMEM)


def cost(flops, moved):
    return pl.CostEstimate(flops=flops, bytes_accessed=moved, transcendentals=0)


def params():
    return pltpu.CompilerParams(vmem_limit_bytes=VMEM_LIMIT)


def exchange_order(count):
    order = [index ^ 1 for index in range(count)][::-1]
    order = order[2:] + order[:2]
    return order[1::-1] + order[2:]


def member_at(position, count):
    member = jnp.zeros_like(position)
    for place, index in enumerate(exchange_order(count)):
        member = jnp.where(position == place, index, member)
    return member


def in_hbm(array):
    return pltpu.with_memory_space_constraint(array, pltpu.HBM)


def in_vmem(array):
    return pltpu.with_memory_space_constraint(array, pltpu.VMEM)


def iota(shape, axis):
    return lax.broadcasted_iota(jnp.int32, shape, axis)


def edge_shape(field_edges, levels, lon):
    pieces = max(p for p in range(1, 8 // levels + 1) if lon // LANES % p == 0)
    return 8, field_edges // 8 * lon + lon // pieces


def write_edges(ref, edges, field_edges, levels):
    lon = edges.shape[1]
    groups = field_edges // 8
    for group in range(groups):
        part = edges[group * 8 : group * 8 + 8]
        ref[:, group * lon : (group + 1) * lon] = part.astype(jnp.bfloat16)
    width = ref.shape[1] - groups * lon
    courant = edges[field_edges : field_edges + levels]
    parts = [courant[:, at : at + width] for at in range(0, lon, width)]
    rest = 8 - len(parts) * levels
    if rest:
        parts.append(jnp.zeros((rest, width), jnp.float32))
    ref[:, groups * lon :] = jnp.concatenate(parts, axis=0).astype(jnp.bfloat16)


def read_edges(ref, field_edges, levels, lon):
    groups = field_edges // 8
    edges = ref[...].astype(jnp.float32)
    fields = [edges[:, group * lon : (group + 1) * lon] for group in range(groups)]
    width = edges.shape[1] - groups * lon
    courant = [
        edges[part * levels : (part + 1) * levels, groups * lon :] for part in range(lon // width)
    ]
    return fields, jnp.concatenate(courant, axis=1)


def write_stencil(stencil_ref, field_count, levels, rows):
    count = field_count * levels * rows
    speed_count = levels * rows
    lat = lax.axis_index("lat")
    lats = lax.axis_size("lat")
    odd = lat % 2

    own = (field_count + 1) * speed_count
    field_edges = field_count * levels * WIDTH
    column = iota((1, stencil_ref.shape[1]), 1)
    edge = column - own
    speed_edge = edge - 2 * field_edges
    is_own, is_speed = edge < 0, speed_edge >= 0
    far = jnp.where(is_speed, speed_edge // levels, edge // field_edges)
    field_edge = edge - far * field_edges
    edge_block = jnp.where(
        is_speed, speed_edge - far * levels + field_count * levels, field_edge // WIDTH
    )
    sides = jnp.where((lat > 0) & (lat < lats - 1), 2, 1)
    block = jnp.where(is_own, column // rows, jnp.where(far < sides, edge_block, -1))
    high = (odd + far + 1) % 2
    edge_place = jnp.where(is_speed, high * (rows + 1) - 1, field_edge % WIDTH - WIDTH + high * (rows + WIDTH))
    place = jnp.where(is_own, column % rows, edge_place)

    def relation(height, first_block):
        line = iota((height, 1), 0)
        line_block = line // rows
        row = line - line_block * rows
        return row, place - row, block == line_block + first_block

    def near_face(here, shift):
        return (here == shift) | (here == shift - 1)

    _, here, same = relation(count, 0)
    for side in range(2):
        outer = (here == side + 1) | (here == side - 2)
        value = jnp.where(near_face(here, side), 7.0, jnp.where(outer, -1.0, 0.0))
        stencil_ref[side * count : (side + 1) * count] = jnp.where(same, value, 0.0).astype(
            jnp.bfloat16
        )
    row, here, same = relation(speed_count, field_count * levels)
    live = ((row > 0) | (lat > 0), (row < rows - 1) | (lat < lats - 1))
    for side in range(2):
        first = 2 * count + side * speed_count
        value = jnp.where(same & near_face(here, side) & live[side], 0.5, 0.0)
        stencil_ref[first : first + speed_count] = value.astype(jnp.bfloat16)


def write_band_matrix(band_matrix_ref, polar_ref, mask_ref, band_ref, weight_ref, rows, levels):
    polar_row = iota(polar_ref.shape, 0)
    polar = jnp.zeros(polar_ref.shape, jnp.int32)
    for index in range(rows):
        polar = jnp.where(polar_row == index, mask_ref[:, index : index + 1], polar)
    polar_ref[...] = polar

    band_width, level_total = weight_ref.shape[1:]
    total = level_total * rows

    def level_at(index):
        place = index // rows
        position = place // levels
        return (member_at(position, level_total // levels) - position) * levels + place

    out_row, in_row = iota((total, 1), 0), iota((1, total), 1)
    of_row = level_at(out_row) == iota((1, level_total), 1)

    def spread(table):
        whole = jnp.concatenate([table] * level_total, axis=0)
        return jnp.sum(jnp.where(of_row, whole, jnp.zeros_like(whole)), axis=1, keepdims=True)

    start = spread(jnp.broadcast_to(band_ref[...], (rows, level_total)))
    offset = level_at(in_row) - start
    matrix = jnp.zeros((total, total), jnp.float32)
    for band in range(band_width):
        matrix = jnp.where(offset == band, spread(weight_ref[:, band, :]), matrix)
    matrix = jnp.where(in_row % rows == out_row % rows, matrix, 0.0)
    for part in range(PARTS):
        rounded = matrix.astype(jnp.bfloat16)
        band_matrix_ref[part * total : (part + 1) * total] = rounded
        matrix = matrix - rounded.astype(jnp.float32)


def edges_body(
    filter_hbm, fields_hbm, courant_hbm, mask_hbm, band_hbm, weight_hbm,
    near_ref, far_ref, stack_ref, stencil_ref, polar_ref, band_matrix_ref,
    mask_ref, band_ref, weight_ref, sems,
    *, field_count, levels, rows
):
    own = stack_ref.shape[0]
    blocks = own // rows
    field_rows = field_count * levels * rows
    pairs = (
        (weight_hbm, weight_ref),
        (band_hbm, band_ref),
        (mask_hbm, mask_ref),
        (fields_hbm, stack_ref.at[pl.ds(0, field_rows)]),
        (courant_hbm, stack_ref.at[pl.ds(field_rows, own - field_rows)]),
    )
    copies = [
        pltpu.make_async_copy(source, target, sems.at[index])
        for index, (source, target) in enumerate(pairs)
    ]
    for copy in copies:
        copy.start()
    odd = lax.axis_index("lat") % 2
    edge = iota((2 * EDGE_ROWS, 1), 0)
    far = (edge >= EDGE_ROWS).astype(jnp.int32)
    inner = edge - far * EDGE_ROWS
    high = (odd + far + 1) % 2
    field_edges = field_count * levels * WIDTH
    of_field = inner < field_edges
    block = jnp.where(of_field, inner // WIDTH, inner - field_edges + field_count * levels)
    row = jnp.where(of_field, inner % WIDTH + high * (rows - WIDTH), high * (rows - 1))
    wanted = jnp.where(block < blocks, block * rows + row, -1)
    pick = jnp.where(iota((2 * EDGE_ROWS, own), 1) == wanted, 1.0, 0.0).astype(jnp.bfloat16)
    write_stencil(stencil_ref, field_count, levels, rows)
    for copy in copies[:3]:
        copy.wait()
    write_band_matrix(band_matrix_ref, polar_ref, mask_ref, band_ref, weight_ref, rows, levels)
    for copy in copies[3:]:
        copy.wait()
    edges = jnp.dot(pick, stack_ref[...], preferred_element_type=jnp.float32)
    write_edges(near_ref, edges[:EDGE_ROWS], field_edges, levels)
    for member in range(2):
        write_edges(far_ref.at[member], edges[EDGE_ROWS:], field_edges, levels)


def tiles(field_count, levels, lon, units):
    for field in range(field_count):
        for part in range(lon // LANES):
            unit = field * (lon // LANES) + part
            for level in range(levels):
                yield field, level, part * LANES, (unit // units, unit % units, level)


def transport_body(
    near_ref, far_ref, stack_ref, stencil_ref, filter_ref, polar_ref, out_ref, *, field_count
):
    pieces, units, levels, rows, _ = out_ref.shape
    lon = stack_ref.shape[1]
    count = field_count * levels * rows
    speed_count = levels * rows
    field_edges = field_count * levels * WIDTH
    near_fields, near_courant = read_edges(near_ref, field_edges, levels, lon)
    partner = lax.axis_index("lat") % 2
    far_fields, far_courant = read_edges(far_ref.at[partner], field_edges, levels, lon)
    rest = EDGE_ROWS // 2 - 2 * levels
    speeds = [near_courant, far_courant, jnp.zeros((rest, lon), jnp.float32)]
    edges = jnp.concatenate(
        near_fields + far_fields + [jnp.concatenate(speeds, axis=0)], axis=0
    )
    source = jnp.concatenate([stack_ref[...], edges.astype(jnp.bfloat16)], axis=0)
    values = jnp.dot(stencil_ref[...], source, preferred_element_type=jnp.float32)
    speed_low = values[2 * count : 2 * count + speed_count] * (1.0 / 12.0)
    speed_high = values[2 * count + speed_count :] * (1.0 / 12.0)
    parts = []
    for first in range(0, count, speed_count):
        flux_low = speed_low * values[first : first + speed_count]
        flux_high = speed_high * values[count + first : count + first + speed_count]
        own = stack_ref[first : first + speed_count].astype(jnp.float32)
        parts.append(own - (flux_high - flux_low))
    moved = jnp.concatenate(parts, axis=0)

    def write(filtered):
        for field, level, at, place in tiles(field_count, levels, lon, units):
            first = (field * levels + level) * rows
            tile = filtered[first : first + rows, at : at + LANES]
            out_ref[place] = tile.astype(jnp.bfloat16)
        for unit in range(field_count * lon // LANES, pieces * units):
            out_ref[unit // units, unit % units] = jnp.zeros(out_ref.shape[2:], jnp.bfloat16)

    polar = polar_ref[...] == 1
    any_polar = jnp.max(polar_ref[...]) == 1

    @pl.when(any_polar)
    def _():
        correction = jnp.dot(
            moved.astype(jnp.bfloat16), filter_ref[...], preferred_element_type=jnp.float32
        )
        wide = jnp.concatenate([polar] * (lon // LANES), axis=1)
        whole = jnp.concatenate([wide] * (field_count * levels), axis=0)
        write(moved + jnp.where(whole, correction, 0.0))

    @pl.when(jnp.logical_not(any_polar))
    def _():
        write(moved)


def remap_body(band_matrix_ref, source_ref, out_ref):
    pieces, units, levels, rows, _ = source_ref.shape
    total = pieces * levels * rows
    columns = jnp.concatenate(
        [
            source_ref[:, unit].astype(jnp.float32).reshape(total, LANES).astype(jnp.bfloat16)
            for unit in range(units)
        ],
        axis=1,
    )
    split = jnp.dot(band_matrix_ref[...], columns, preferred_element_type=jnp.float32)
    result = split[(PARTS - 1) * total :]
    for part in range(PARTS - 1)[::-1]:
        result = result + split[part * total : (part + 1) * total]
    for unit in range(units):
        part = result[:, unit * LANES : (unit + 1) * LANES]
        out_ref[:, unit] = part.reshape(pieces, levels, rows, LANES).astype(jnp.bfloat16)


def collect_body(source_ref, out_hbm, out_ref, sems):
    field_count, levels, _, lon = out_ref.shape
    units = source_ref.shape[1]
    copies = []
    for field, level, at, place in tiles(field_count, levels, lon, units):
        out_ref[field, level, :, at : at + LANES] = source_ref[place]
        if at + LANES == lon and level == levels - 1:
            copy = pltpu.make_async_copy(out_ref.at[field], out_hbm.at[field], sems.at[field])
            copy.start()
            copies.append(copy)
    for copy in copies:
        copy.wait()


def on_device(fields, courant, filter_matrix, polar_mask, band_start, remap_weights):
    def array(*shape, dtype=jnp.bfloat16):
        return jax.ShapeDtypeStruct(shape, dtype)

    field_count, levels, rows, lon = fields.shape
    lats, levs = lax.axis_size("lat"), lax.axis_size("lev")
    level_total, band_width = remap_weights.shape[1:]
    if lon % LANES or rows % 8:
        raise ValueError("uneven tiles")
    units = -(-(field_count * lon // LANES) // levs)
    count = field_count * levels * rows
    blocks = (field_count + 1) * levels
    own = blocks * rows
    field_edges = field_count * levels * WIDTH
    if field_edges % 8 or 8 % levels or field_edges + levels > EDGE_ROWS:
        raise ValueError("uneven edges")
    edges = array(*edge_shape(field_edges, levels, lon))
    total = level_total * rows

    hbm = pl.BlockSpec(memory_space=pltpu.HBM)
    sizes = dict(field_count=field_count, levels=levels, rows=rows)
    small = [
        polar_mask.reshape(1, -1),
        band_start.reshape(1, -1),
        jnp.swapaxes(remap_weights, 1, 2),
    ]
    inputs = [filter_matrix, fields.reshape(count, lon), courant.reshape(own - count, lon), *small]
    near, far, stack, stencil, polar, band_matrix = pl.pallas_call(
        functools.partial(edges_body, **sizes),
        out_shape=(
            edges,
            array(2, *edges.shape),
            array(own, lon),
            array(2 * (count + levels * rows), own + 2 * field_edges + EDGE_ROWS // 2),
            array(rows, LANES, dtype=jnp.int32),
            array(PARTS * total, total),
        ),
        in_specs=[hbm] * len(inputs),
        out_specs=(WHOLE,) * 6,
        scratch_shapes=[pltpu.VMEM(each.shape, each.dtype) for each in small]
        + [pltpu.SemaphoreType.DMA((len(inputs) - 1,))],
        compiler_params=params(),
        cost_estimate=cost(2 * own * own * lon, 4 * own * lon),
    )(*map(in_hbm, inputs))

    near_pairs = [(i, i + 1) for i in range(0, lats - 1, 2)]
    from_near = lax.ppermute(
        near, "lat", near_pairs + [(target, source) for source, target in near_pairs]
    )
    far_groups = [[i, i + 1] for i in range(1, lats - 1, 2)] + [[0, lats - 1]]

    def exchange_far(array):
        return lax.all_to_all(
            array, "lat", split_axis=0, concat_axis=0, tiled=True, axis_index_groups=far_groups
        )

    lat_index = lax.axis_index("lat")
    has_far = (lat_index > 0) & (lat_index < lats - 1)
    from_far = lax.cond(has_far, exchange_far, lambda array: array, far)

    pieces = pl.pallas_call(
        functools.partial(transport_body, field_count=field_count),
        out_shape=array(levs, units, levels, rows, LANES),
        in_specs=[WHOLE] * 6,
        out_specs=WHOLE,
        compiler_params=params(),
        cost_estimate=cost(2 * count * lon * lon, 2 * lon * lon),
    )(from_near, from_far, stack, stencil, in_vmem(filter_matrix), polar)

    def exchange(array):
        group = exchange_order(levs)
        return lax.all_to_all(
            array, "lev", split_axis=0, concat_axis=0, tiled=True, axis_index_groups=[group]
        )

    remapped = pl.pallas_call(
        remap_body,
        out_shape=array(*pieces.shape),
        in_specs=[WHOLE] * 2,
        out_specs=WHOLE,
        compiler_params=params(),
        cost_estimate=cost(6 * total * total * units * LANES, 4 * total * units * LANES),
    )(band_matrix, exchange(pieces))
    return pl.pallas_call(
        collect_body,
        out_shape=array(*fields.shape),
        in_specs=[WHOLE],
        out_specs=hbm,
        scratch_shapes=[
            pltpu.VMEM(fields.shape, fields.dtype),
            pltpu.SemaphoreType.DMA((field_count,)),
        ],
        compiler_params=params(),
        cost_estimate=cost(count * lon, 4 * count * lon),
    )(exchange(remapped))


def solution(mesh):
    return jax.shard_map(
        on_device,
        mesh=mesh,
        in_specs=(
            P(None, "lev", "lat", None),
            P("lev", "lat", None),
            P(),
            P("lat"),
            P(),
            P("lat", None, None),
        ),
        out_specs=P(None, "lev", "lat", None),
        check_vma=False,
    )
```
